32 devices in a mesh: groups: 2 (over x), shard: 16 (over z, y, core).
Axes of the slice: x: 2, y: 2, z: 4, core: 2. Of those that a mesh axis runs over, the one named last changes fastest.
Arguments:
- embeddings: bfloat16 [16384, 1024], P(('groups', 'shard')), parts along dimension 0, may hold values from -6 to 6
- scales: bfloat16 [16384], P(('groups', 'shard')), parts along dimension 0, may hold values from 0.039794922 to 0.119628906
- cluster: int32 [16384, 1], P(('groups', 'shard')), parts along dimension 0, may hold values from 0 to 15; in each aligned block of 512 rows (0 to 511, 512 to 1023, ...) at most 64 rows name the same one
- pair_listed: int32 [32, 5], P(('groups', 'shard')), parts along dimension 0, may hold values from 0 to 1, as said below
Outputs:
- best: float32 [16384], P(('groups', 'shard')), parts along dimension 0
The draws below stay inside these ranges and needn't reach their ends.
There are 2 independent parts, one for each index of `groups`. The reference program is written for one: setup_inputs(seed, part) draws one part's arguments, and reference() takes and returns one part's arrays. A program takes and returns all parts, laid end to end along the dimension named above; each array names one. Nothing has to cross between parts.
Inputs may be any that keep to these rules, and one draw needn't show every extreme that they name: In each shard's 512 rows at most 64 rows name one sub-cluster, and every sub-cluster is named by some row of the group. `pair_listed`: column 0 is 1 for every a < 15; entries with a + k + 1 >= 16 are 0.
All inputs are finite; a program needn't handle non-finite values.
Results may differ from the reference program's by a relative error of at most 0.0003.
Values may be sent and summed in bfloat16 or wider, within the bound.
No kernel may reach another device: no remote copies, remote signals or barrier semaphores. Data moves between devices by JAX's collectives and lax.ppermute only.
A program may use at most 64 MiB of HBM per device.

```python
import math
import jax
import jax.numpy as jnp
import numpy as np
from jax import lax

D = 1024
ROWS_DEV = 512
PARTNERS = 5
SUBC = 16
CAP = 64
SLOTS = 1024
ROWS = 8192
N_SHARD = 16


def draw_pair_listed(key, part):
    coin = jax.random.randint(jax.random.fold_in(key, 17), (SUBC, PARTNERS), 0, 2, dtype=jnp.int32)
    column = jnp.arange(PARTNERS, dtype=jnp.int32)[None, :]
    source = jnp.arange(SUBC, dtype=jnp.int32)[:, None]
    listed = jnp.where(column == 0, 1, coin)
    return jnp.where(source + column + 1 < SUBC, listed, 0).astype(jnp.int32)


def block_scale(stream_key, extent, cuts, smallest, largest):
    loudness, own = 1.0, jax.random.fold_in(stream_key, 6)
    for dim, parts in cuts:
        steps = jnp.exp(jax.random.uniform(jax.random.fold_in(own, dim), (parts,), jnp.float32, smallest / len(cuts), largest / len(cuts)))
        loudness = loudness * jnp.repeat(steps, extent[dim] // parts).reshape([-1 if axis == dim else 1 for axis in range(len(extent))])
    return loudness


def routed_block(stream_key, own, number, rows, amount, top, most, slope):
    ranking = jax.random.permutation(stream_key, amount)
    packed, usual = load_shares(amount, rows * top, most, slope, True), load_shares(amount, rows * top, most, slope, False)
    places = jnp.arange(amount)

    def named(lengths, rotation):
        used = int((lengths > 0).sum())
        fixed = max(1, used // 4)
        moved = fixed + (places - fixed + rotation * (used - fixed)) % max(1, amount - fixed)
        return jnp.zeros((amount,), jnp.int32).at[ranking[jnp.where(places < fixed, places, moved)]].set(jnp.asarray(lengths, jnp.int32))

    lengths = jnp.where(number % 4 == 0, named(packed, number // 4), named(usual, number - number // 4 - 1))
    mixed = jax.random.permutation(jax.random.fold_in(own, 3), amount)
    giver, taker = mixed[0:amount // 2 * 2:2], mixed[1:amount // 2 * 2:2]
    slack = jnp.minimum(lengths[giver] - 1, most - lengths[taker]) // 2
    slack = jnp.where((giver == ranking[0]) | (taker == ranking[0]) | (lengths[taker] == 0), 0, jnp.maximum(slack, 0))
    moved = jax.random.randint(jax.random.fold_in(own, 4), (amount // 2,), 0, 1 << 20) % (slack + 1)
    lengths = lengths.at[giver].add(-moved).at[taker].add(moved)
    items = jnp.searchsorted(jnp.cumsum(lengths), jnp.arange(rows * top), side="right").astype(jnp.int32)
    grid = items.reshape(top, rows).T
    grid = grid[jax.random.permutation(jax.random.fold_in(own, 1), rows)]
    rotation = jax.random.randint(jax.random.fold_in(own, 2), (rows, 1), 0, top)
    return jnp.take_along_axis(grid, (jnp.arange(top)[None, :] + rotation) % top, axis=1)


def load_shares(count, total, most, skew, full):
    portions = [(1 << 20) // math.isqrt(grade ** skew) + 1 for grade in range(1, count + 1)]
    largest = most if full else min(most, max(-(-total // count), total * portions[0] // sum(portions)))
    least = 1 if total - largest >= count - 1 else 0
    counts, spare = [largest] + [least] * (count - 1), total - largest - least * (count - 1)
    while spare > 0:
        free = [i for i in range(1, count) if counts[i] < largest] or [i for i in range(1, count) if counts[i] < most]
        whole, left = sum([portions[i] for i in free]), spare
        for i in free:
            extra = min(most - counts[i], max(1, left * portions[i] // whole), spare)
            counts[i] = counts[i] + extra
            spare = spare - extra
    return np.array(counts)


def gaussian(own_key, dims, width, bound, cuts=(), kind=jnp.bfloat16):
    level = block_scale(own_key, dims, cuts, -0.22, 0.18) if cuts else 1.0
    array = jax.random.normal(own_key, dims, jnp.float32) * width * level
    return jnp.minimum(jnp.maximum(array, -bound), bound).astype(kind)


def setup_inputs(seed: int = 0, part: int = 0) -> dict:
    key_list = jax.random.split(jax.random.key(seed), 5)
    part_splits = jax.random.split(jax.random.fold_in(key_list[4], part), 5)
    embeddings = gaussian(part_splits[0], (ROWS, D), 1.0, 6.0, ((0, 16),))
    scales = jnp.clip(jnp.exp(math.log(0.119628906) - 1.1006552 * jax.random.uniform(part_splits[1], (ROWS,), jnp.float32) ** block_scale(part_splits[1], (ROWS,), ((0, 16),), -0.2, 0.2)), 0.039794922, 0.119628906).astype(jnp.bfloat16)
    cluster_keys = jax.random.split(jax.random.fold_in(part_splits[2], 1), ROWS // ROWS_DEV)
    cluster_turns = jax.random.permutation(jax.random.fold_in(part_splits[2], 3), ROWS // ROWS_DEV)
    cluster = jax.vmap(lambda own, number: routed_block(jax.random.fold_in(part_splits[2], 2), own, number, ROWS_DEV, SUBC, 1, CAP, 2))(cluster_keys, cluster_turns).reshape((ROWS, 1))
    pair_listed = draw_pair_listed(jax.random.fold_in(jax.random.fold_in(key_list[4], part), 71), part)
    return {"embeddings": embeddings, "scales": scales, "cluster": cluster, "pair_listed": pair_listed}


def slot_positions(cluster):
    shard_cluster = cluster.reshape(N_SHARD, ROWS_DEV)
    onehot = (shard_cluster[:, :, None] == jnp.arange(SUBC, dtype=jnp.int32)[None, None, :]).astype(jnp.int32)
    before = jnp.cumsum(onehot, axis=1) - onehot
    within = jnp.sum(before * onehot, axis=2)
    source = jnp.arange(N_SHARD, dtype=jnp.int32)[:, None] * CAP
    return (within + source).reshape(-1).astype(jnp.int32)


def scaled_tile(left, left_scale, right, right_scale):
    raw = lax.dot_general(left, right, (((1,), (1,)), ((), ())), preferred_element_type=jnp.float32)
    return raw * left_scale.astype(jnp.float32)[:, None] * right_scale.astype(jnp.float32)[None, :]


def reference(embeddings, scales, cluster, pair_listed):
    target = cluster[:, 0].astype(jnp.int32)
    position = slot_positions(target)
    blocks = jnp.zeros((SUBC, SLOTS, D), jnp.bfloat16).at[target, position].set(embeddings)
    block_scales = jnp.zeros((SUBC, SLOTS), jnp.bfloat16).at[target, position].set(scales)
    lowest = jnp.float32(-jnp.inf)
    diagonal = jnp.arange(SLOTS, dtype=jnp.int32)[:, None] == jnp.arange(SLOTS, dtype=jnp.int32)[None, :]

    def per_block(index):
        left = blocks[index]
        left_scale = block_scales[index]
        live_left = left_scale != 0
        scores = scaled_tile(left, left_scale, left, left_scale)
        keep = live_left[None, :] & jnp.logical_not(diagonal)
        row_best = jnp.max(jnp.where(keep, scores, lowest), axis=1)
        columns = []
        for step in range(PARTNERS):
            other = index + step + 1
            inside = other < SUBC
            clamped = jnp.minimum(other, SUBC - 1).astype(jnp.int32)
            right = blocks[clamped]
            right_scale = block_scales[clamped]
            listed = (pair_listed[index, step] == 1) & inside
            scores = scaled_tile(left, left_scale, right, right_scale)
            live = listed & live_left[:, None] & (right_scale != 0)[None, :]
            masked = jnp.where(live, scores, lowest)
            row_best = jnp.maximum(row_best, jnp.max(masked, axis=1))
            columns.append(jnp.max(masked, axis=0))
        return row_best, jnp.stack(columns)

    rows_best, cols_best = lax.map(per_block, jnp.arange(SUBC, dtype=jnp.int32))
    slot_best = rows_best
    for step in range(PARTNERS):
        offset = step + 1
        filler = jnp.full((offset, SLOTS), lowest, jnp.float32)
        moved = jnp.concatenate([filler, cols_best[:SUBC - offset, step]], axis=0)
        slot_best = jnp.maximum(slot_best, moved)
    return slot_best[target, position]
```

```python
import functools

import jax
import jax.numpy as jnp
from jax import lax
from jax.experimental import pallas as pl
from jax.experimental.pallas import tpu as pltpu
from jax.sharding import PartitionSpec as P

LOWEST = float("-inf")
WORD = 31
LANES = 128


def meet_kernel(words, sides, diagonal, chunk, count, known, *refs):
    index, moving = refs[0], refs[1]
    blocks = refs[2 : 2 + count]
    scale, ones, bits = refs[2 + count : 5 + count]
    before = dict(zip(known, refs[5 + count :]))
    outs = list(refs[5 + count + len(known) :])
    column = outs.pop() if "column" in sides else None
    rows = moving.shape[0]
    who = index[0]

    def along_sublanes(value):
        return jnp.transpose(jnp.broadcast_to(value, (LANES, rows)))

    own_scale = along_sublanes(scale[pl.ds(who, 1), :])
    own_bits = [along_sublanes(bits[pl.ds(who * words + w, 1), :]) for w in range(words)]
    best = None
    for j, block in enumerate(blocks):
        other = index[1 + j]
        other_scale = scale[pl.ds(other, 1), :]
        other_ones = [ones[pl.ds(other * words + w, 1), :] for w in range(words)]
        for first in range(0, block.shape[0], chunk):
            raw = lax.dot_general(
                moving[...],
                block[first : first + chunk, :],
                (((1,), (1,)), ((), ())),
                preferred_element_type=jnp.float32,
            )
            for at in range(0, chunk, LANES):
                here = slice(first + at, first + at + LANES)
                scores = raw[:, at : at + LANES] * own_scale * other_scale[:, here]
                shared = own_bits[0] & other_ones[0][:, here]
                for w in range(1, words):
                    shared = shared | (own_bits[w] & other_ones[w][:, here])
                keep = shared != 0
                if diagonal and j == 0:
                    row = lax.broadcasted_iota(jnp.int32, scores.shape, 0)
                    lane = lax.broadcasted_iota(jnp.int32, scores.shape, 1) + (first + at)
                    keep = keep & (row != lane)
                scores = jnp.where(keep, scores, LOWEST)
                if "row" in sides:
                    found = jnp.max(scores, axis=0, keepdims=True)
                    if j in before:
                        found = jnp.maximum(found, before[j][:, here])
                    outs[j][:, here] = found
                if column is not None:
                    best = scores if best is None else jnp.maximum(best, scores)
    if column is not None:
        column[...] = jnp.max(jnp.transpose(best), axis=0, keepdims=True)


def meet(index, moving, blocks, scale, ones, bits, words, sides, before={}, diagonal=False):
    rows, width = moving.shape
    count = len(blocks)
    chunk = min(256, rows)
    outs = []
    if "row" in sides:
        outs += [jax.ShapeDtypeStruct((1, rows), jnp.float32)] * count
    if "column" in sides:
        outs += [jax.ShapeDtypeStruct((1, rows), jnp.float32)]
    vmem = pl.BlockSpec(memory_space=pltpu.VMEM)
    return pl.pallas_call(
        functools.partial(meet_kernel, words, sides, diagonal, chunk, count, tuple(before)),
        out_shape=outs,
        in_specs=[pl.BlockSpec(memory_space=pltpu.SMEM)] + [vmem] * (count + 4 + len(before)),
        out_specs=[vmem] * len(outs),
        compiler_params=pltpu.CompilerParams(vmem_limit_bytes=20 * 2**20),
        cost_estimate=pl.CostEstimate(
            flops=2 * rows * rows * count * width,
            bytes_accessed=2 * rows * width * (count + 1),
            transcendentals=0,
        ),
    )(index, moving, *blocks, scale, ones, bits, *before.values())


def pair_words(listed, subclusters, words):
    source = jnp.arange(subclusters, dtype=jnp.int32)
    met = source[:, None] == source[None, :]
    ahead = source[None, :] - source[:, None]
    for k in range(listed.shape[1]):
        forward = (ahead == k + 1) & (listed[:, k] == 1)[:, None]
        backward = (ahead == -k - 1) & (listed[:, k] == 1)[None, :]
        met = met | forward | backward
    table = []
    for w in range(words):
        weight = jnp.where(source // WORD == w, jnp.int32(1) << (source % WORD), 0)
        table.append(jnp.sum(jnp.where(met, weight[None, :], 0), axis=1))
    return table


def per_device(embeddings, scales, cluster, pair_listed):
    rows, width = embeddings.shape
    shards = lax.axis_size("shard")
    here = lax.axis_index("shard")
    plane = 1
    while plane * plane * 4 <= shards:
        plane *= 2
    planes = shards // plane
    half = planes // 2
    owned, partners = pair_listed.shape
    subclusters = shards * owned
    words = -(-subclusters // WORD)

    order = [place // 2 + (place % 2) * half for place in range(planes)]
    place_of = [order.index(z) for z in range(planes)]

    def permuted(value, target):
        return lax.ppermute(value, "shard", [(s, target(s)) for s in range(shards)])

    def across(bit):
        return lambda s: s ^ bit

    def along(distance):
        def target(s):
            z = order[(place_of[s // plane] + distance) % planes]
            return z * plane + s % plane

        return target

    def sender_of(distance):
        table = [0] * shards
        for s in range(shards):
            table[along(distance)(s)] = s
        return jnp.asarray(table, jnp.int32)[here]

    arrived = {}
    for distance in range(half, 0, -1):
        arrived[distance] = permuted(embeddings, along(distance))
    held = {0: embeddings}
    bit = plane // 2
    while bit:
        for j in sorted(held):
            held[j | bit] = permuted(held[j], across(bit))
        bit //= 2
    blocks = [held[j] for j in range(plane)]

    pairs = jnp.pad(pair_listed.reshape(-1), (0, -(owned * partners) % LANES))
    info = jnp.concatenate(
        [scales.astype(jnp.float32), cluster[:, 0].astype(jnp.float32), pairs.astype(jnp.float32)]
    )
    everyone = lax.all_to_all(
        jnp.broadcast_to(info[None, :], (shards, info.shape[0])),
        "shard",
        split_axis=0,
        concat_axis=0,
        tiled=True,
    )
    scale = everyone[:, :rows]
    named = everyone[:, rows : 2 * rows].astype(jnp.int32)
    listed = everyone[:, 2 * rows : 2 * rows + owned * partners].astype(jnp.int32)
    table = pair_words(listed.reshape(subclusters, partners), subclusters, words)
    source = jnp.arange(subclusters, dtype=jnp.int32)
    same = named[:, None, :] == source[None, :, None]
    ones = jnp.stack(
        [jnp.where(named // WORD == w, jnp.int32(1) << (named % WORD), 0) for w in range(words)], axis=1
    ).reshape(shards * words, rows)
    bits = jnp.stack(
        [jnp.sum(jnp.where(same, table[w][None, :, None], 0), axis=1) for w in range(words)], axis=1
    ).reshape(shards * words, rows)

    mates = here ^ jnp.arange(plane, dtype=jnp.int32)

    def index_of(mover):
        return jnp.concatenate([mover[None], mates])

    [own] = meet(index_of(here), embeddings, blocks, scale, ones, bits, words, ("column",), diagonal=True)
    gathered = {0: own}
    returned = []
    for distance in range(half, 0, -1):
        two_sided = 2 * distance != planes
        found = meet(
            index_of(sender_of(distance)),
            arrived[distance],
            blocks,
            scale,
            ones,
            bits,
            words,
            ("row", "column") if two_sided else ("row",),
            gathered,
        )
        if two_sided:
            returned.append(permuted(found[plane], along(-distance)))
        gathered = dict(enumerate(found[:plane]))
    returned += [permuted(gathered[j], across(j)) for j in range(plane - 1, 0, -1)]
    result = functools.reduce(jnp.maximum, returned, gathered[0])
    return result.reshape(rows)


def solution(mesh):
    placed = (
        P(("groups", "shard"), None),
        P(("groups", "shard")),
        P(("groups", "shard"), None),
        P(("groups", "shard"), None),
    )
    return jax.shard_map(
        per_device, mesh=mesh, in_specs=placed, out_specs=P(("groups", "shard")), check_vma=False
    )
```

```python
import functools

import jax
import jax.numpy as jnp
from jax import lax
from jax.experimental import pallas as pl
from jax.experimental.pallas import tpu as pltpu
from jax.sharding import PartitionSpec as P

LOWEST = float("-inf")
WORD = 16
LANES = 128
SUBLANES = 8
STRIP = 64
VMEM_RAW = 24 * 2**20
VMEM_CALL = 40 * 2**20


def product_kernel(moving, *refs):
    blocks, out = refs[:-1], refs[-1]
    rows = moving.shape[0]
    chunk = min(256, rows)
    for j, block in enumerate(blocks):
        for first in range(0, rows, chunk):
            out[:, j * rows + first : j * rows + first + chunk] = lax.dot_general(
                moving[...],
                block[first : first + chunk, :],
                (((1,), (1,)), ((), ())),
                preferred_element_type=jnp.float32,
            )


def products(moving, blocks):
    rows, width = moving.shape
    vmem = pl.BlockSpec(memory_space=pltpu.VMEM)
    return pl.pallas_call(
        product_kernel,
        out_shape=jax.ShapeDtypeStruct((rows, len(blocks) * rows), jnp.float32),
        in_specs=[vmem] * (1 + len(blocks)),
        out_specs=vmem,
        compiler_params=pltpu.CompilerParams(vmem_limit_bytes=VMEM_CALL),
        cost_estimate=pl.CostEstimate(
            flops=2 * rows * rows * len(blocks) * width,
            bytes_accessed=2 * rows * width * (len(blocks) + 1),
            transcendentals=0,
        ),
    )(moving, *blocks)


def maxima_kernel(partners, count, kinds, carried, index, device, everyone, *refs):
    raws = refs[: len(kinds)]
    before = refs[len(kinds) : len(kinds) + carried]
    row_outs = refs[len(kinds) + carried : len(kinds) + carried + count]
    column_outs = list(refs[len(kinds) + carried + count : -1])
    strip_best = refs[-1]
    rows = raws[0].shape[0]
    strip = min(STRIP, rows)
    per_block = rows // LANES
    groups = count * per_block

    shards = everyone.shape[0]
    words = -(-shards // WORD)
    source = device[...]
    table = pair_words(everyone[:, 2 * rows :], source, partners, words)

    def scale_of(at):
        return everyone[at : at + 1, 0:rows]

    def cluster_of(at):
        return everyone[at : at + 1, rows : 2 * rows].astype(jnp.int32)

    def bits_of(at):
        named = cluster_of(at) == source
        return [jnp.sum(jnp.where(named, t, 0.0), axis=0, keepdims=True).astype(jnp.int32) for t in table]

    def ones_of(at):
        named = cluster_of(at)
        return [jnp.where(named // WORD == w, jnp.int32(1) << (named % WORD), 0) for w in range(words)]

    def along_sublanes(value):
        return jnp.transpose(jnp.broadcast_to(value, (LANES, rows)))

    lane_scale = [scale_of(index[j]) for j in range(count)]
    lane_ones = [ones_of(index[j]) for j in range(count)]

    def lanes_of(per, g):
        first = g % per_block * LANES
        return per[g // per_block][:, first : first + LANES]

    row_part = [None] * groups
    own_best = None
    for r, (same, wants_row, wants_column) in enumerate(kinds):
        who = index[count + r]
        mine = scale_of(who)
        mine_down = along_sublanes(mine)
        bits_down = [along_sublanes(b) for b in bits_of(who)]
        for first in range(0, rows, strip):
            here = slice(first, first + strip)
            best = None
            for g in range(groups):
                value = raws[r][here, g * LANES : (g + 1) * LANES]
                met = bits_down[0][here] & lanes_of([o[0] for o in lane_ones], g)
                for w in range(1, words):
                    met = met | (bits_down[w][here] & lanes_of([o[w] for o in lane_ones], g))
                keep = met != 0
                if same and g < per_block and g * LANES < first + strip and first < (g + 1) * LANES:
                    down = lax.broadcasted_iota(jnp.int32, value.shape, 0) + first
                    across = lax.broadcasted_iota(jnp.int32, value.shape, 1) + g * LANES
                    keep = keep & (down != across)
                if wants_row:
                    value = jnp.where(keep, value * mine_down[here], LOWEST)
                    part = jnp.max(value.reshape(strip // SUBLANES, SUBLANES, LANES), axis=0)
                    row_part[g] = part if row_part[g] is None else jnp.maximum(row_part[g], part)
                    if wants_column:
                        value = value * lanes_of(lane_scale, g)
                else:
                    value = jnp.where(keep, value * lanes_of(lane_scale, g), LOWEST)
                if wants_column:
                    best = value if best is None else jnp.maximum(best, value)
            if wants_column:
                strip_best[here, :] = best
        if wants_column:
            found = jnp.max(jnp.transpose(strip_best[...]), axis=0, keepdims=True)
            if not wants_row:
                found = found * mine
            if same:
                own_best = found
            else:
                column_outs.pop(0)[...] = found
    for j in range(count):
        for at in range(per_block):
            here = slice(at * LANES, (at + 1) * LANES)
            part = row_part[j * per_block + at]
            found = None
            if part is not None:
                found = jnp.max(part, axis=0, keepdims=True) * lane_scale[j][:, here]
            for other in ([own_best] if j == 0 and own_best is not None else []) + ([before[j]] if carried else []):
                found = other[:, here] if found is None else jnp.maximum(found, other[:, here])
            row_outs[j][:, here] = found


def maxima(index, device, everyone, partners, raws, kinds, count, before):
    rows = raws[0].shape[0]
    vmem = pl.BlockSpec(memory_space=pltpu.VMEM)
    columns = sum(column and not same for same, _, column in kinds)
    return pl.pallas_call(
        functools.partial(maxima_kernel, partners, count, tuple(kinds), len(before), index),
        out_shape=[jax.ShapeDtypeStruct((1, rows), jnp.float32)] * (count + columns),
        in_specs=[vmem] * (2 + len(raws) + len(before)),
        out_specs=[vmem] * (count + columns),
        scratch_shapes=[pltpu.VMEM((rows, LANES), jnp.float32)],
        compiler_params=pltpu.CompilerParams(vmem_limit_bytes=VMEM_CALL),
        cost_estimate=pl.CostEstimate(
            flops=8 * rows * rows * count * len(raws),
            bytes_accessed=4 * rows * rows * count * len(raws),
            transcendentals=0,
        ),
    )(device, everyone, *raws, *before)


def pair_words(listed, source, partners, words):
    shards = listed.shape[0]
    lane = lax.broadcasted_iota(jnp.int32, listed.shape, 1)
    target = source + lane + 1
    used = (lane < partners) & (target < shards) & (listed == 1.0)

    def weight(which, w):
        return jnp.where(which // WORD == w, jnp.int32(1) << (which % WORD), 0).astype(jnp.float32)

    table = []
    for w in range(words):
        met = jnp.where(used, weight(target, w), 0.0) + jnp.where(lane == 0, weight(source, w), 0.0)
        met = jnp.sum(met, axis=1, keepdims=True)
        behind = jnp.where(used, weight(source, w), 0.0)
        for i in range(shards):
            hit = jnp.where(target == source[i : i + 1, :], behind, 0.0)
            here = jnp.sum(jnp.sum(hit, axis=0, keepdims=True), axis=1, keepdims=True)
            met = met + jnp.where(lax.broadcasted_iota(jnp.int32, met.shape, 0) == i, here, 0.0)
        table.append(met)
    return table


def joined_kernel(*refs):
    pieces, out = refs[:-2], refs[-1]
    at = 0
    for piece in pieces:
        out[at : at + piece.shape[0], :] = piece[...]
        at += piece.shape[0]


def joined(pieces, after):
    vmem = pl.BlockSpec(memory_space=pltpu.VMEM)
    return pl.pallas_call(
        joined_kernel,
        out_shape=jax.ShapeDtypeStruct((sum(p.shape[0] for p in pieces), pieces[0].shape[1]), jnp.float32),
        in_specs=[vmem] * len(pieces) + [pl.BlockSpec(memory_space=pl.ANY)],
        out_specs=vmem,
        compiler_params=pltpu.CompilerParams(vmem_limit_bytes=2**20),
    )(*pieces, after)


def device_table(shards, plane, planes, order, place_of, here):
    rel = jnp.arange(shards, dtype=jnp.int32)
    place = jnp.sum(jnp.where(jnp.arange(planes) == here // plane, jnp.asarray(place_of, jnp.int32), 0))
    place = (place - rel // plane) % planes
    z = jnp.sum(jnp.where(place[:, None] == jnp.arange(planes)[None, :], jnp.asarray(order, jnp.int32)[None, :], 0), axis=1)
    return (z * plane + (here % plane ^ rel % plane)).reshape(shards, 1)


def per_device(embeddings, scales, cluster, pair_listed):
    rows, width = embeddings.shape
    shards = lax.axis_size("shard")
    here = lax.axis_index("shard")
    plane = 1
    while plane * plane * 4 <= shards:
        plane *= 2
    planes = shards // plane
    half = planes // 2
    owned, partners = pair_listed.shape

    order = [place // 2 + (place % 2) * half for place in range(planes)]
    place_of = [order.index(z) for z in range(planes)]

    def permuted(value, target):
        return lax.ppermute(value, "shard", [(s, target(s)) for s in range(shards)])

    def across(bit):
        return lambda s: s ^ bit

    def along(distance):
        def target(s):
            z = order[(place_of[s // plane] + distance) % planes]
            return z * plane + s % plane

        return target

    arrived = {}
    for distance in range(1, half + 1):
        arrived[distance] = permuted(embeddings, along(distance))
    held = {0: embeddings}
    bit = plane // 2
    while bit:
        for j in sorted(held):
            held[j | bit] = permuted(held[j], across(bit))
        bit //= 2
    blocks = [held[j] for j in range(plane)]

    pairs = jnp.pad(pair_listed.reshape(-1).astype(jnp.float32), (0, -(owned * partners) % LANES))
    told = jnp.concatenate([scales.astype(jnp.float32), cluster[:, 0].astype(jnp.float32), pairs])[None, :]
    pieces, bit = [told], 1
    while bit < plane:
        mine = pieces[0] if len(pieces) == 1 else jnp.concatenate(pieces, axis=0)
        pieces.append(permuted(mine, across(bit)))
        bit *= 2
    raw = products(embeddings, blocks)
    tiles = [(0, raw, (True, False, True))]
    told = joined(pieces, raw)
    everyone = jnp.concatenate([told] + [permuted(told, along(t)) for t in range(1, planes)], axis=0)
    for distance in range(half, 0, -1):
        moving, raw = lax.optimization_barrier((arrived[distance], raw))
        tiles[-1] = (tiles[-1][0], raw, tiles[-1][2])
        raw = products(moving, blocks)
        tiles.append((distance * plane, raw, (False, True, 2 * distance != planes)))
    device = device_table(shards, plane, planes, order, place_of, here)
    at_once = max(1, VMEM_RAW // (4 * rows * rows * plane))
    gathered, columns = [], []
    for first in range(0, len(tiles), at_once):
        part = tiles[first : first + at_once]
        rows_of = tuple(range(plane)) + tuple(tile[0] for tile in part)
        found = maxima(rows_of, device, everyone, partners, [t[1] for t in part], [t[2] for t in part], plane, gathered)
        gathered = found[:plane]
        columns += found[plane:]

    result = gathered[0]
    returned = []
    for distance in range(half - (2 * half == planes), 0, -1):
        returned.append(permuted(columns.pop(0), along(-distance)))
    returned += [permuted(gathered[j], across(j)) for j in range(plane - 1, 0, -1)]
    return functools.reduce(jnp.maximum, returned, result).reshape(rows)


def solution(mesh):
    placed = (
        P(("groups", "shard"), None),
        P(("groups", "shard")),
        P(("groups", "shard"), None),
        P(("groups", "shard"), None),
    )
    return jax.shard_map(
        per_device, mesh=mesh, in_specs=placed, out_specs=P(("groups", "shard")), check_vma=False
    )
```

```python
import functools

import jax
import jax.numpy as jnp
from jax import lax
from jax.experimental import pallas as pl
from jax.experimental.pallas import tpu as pltpu
from jax.sharding import PartitionSpec as P

LOWEST = float("-inf")
WORD = 16
LANES = 128
SUBLANES = 8
STRIP = 64
VMEM_SPARE = 4 * 2**20


def gather_kernel(count, *refs):
    blocks, out, plane, arrived = refs[:count], refs[count], refs[count + 1], refs[count + 2]
    rows = blocks[0].shape[0]
    copies = [
        pltpu.make_async_copy(block, plane.at[j * rows : (j + 1) * rows, :], arrived.at[j])
        for j, block in enumerate(blocks)
    ]
    for copy in copies:
        copy.start()
    for copy in copies:
        copy.wait()
    times_plane(plane.at[:rows, :], plane, out)


def times_plane(moving, plane, out):
    chunk = min(256, moving.shape[0])
    for first in range(0, plane.shape[0], chunk):
        out[:, first : first + chunk] = lax.dot_general(
            moving[...],
            plane[first : first + chunk, :],
            (((1,), (1,)), ((), ())),
            preferred_element_type=jnp.float32,
        )


def cost_of(rows, width, others):
    return pl.CostEstimate(
        flops=2 * rows * others * width, bytes_accessed=2 * (rows + others) * width, transcendentals=0
    )


def gathered_plane(blocks):
    rows, width = blocks[0].shape
    others = rows * len(blocks)
    vmem = pl.BlockSpec(memory_space=pltpu.VMEM)
    return pl.pallas_call(
        functools.partial(gather_kernel, len(blocks)),
        out_shape=[
            jax.ShapeDtypeStruct((rows, others), jnp.float32),
            jax.ShapeDtypeStruct((others, width), blocks[0].dtype),
        ],
        in_specs=[pl.BlockSpec(memory_space=pl.ANY)] * len(blocks),
        out_specs=[vmem, vmem],
        scratch_shapes=[pltpu.SemaphoreType.DMA((len(blocks),))],
        compiler_params=pltpu.CompilerParams(vmem_limit_bytes=4 * rows * others + 2 * others * width + VMEM_SPARE),
        cost_estimate=cost_of(rows, width, others),
    )(*blocks)


def products(moving, plane):
    rows, width = moving.shape
    others = plane.shape[0]
    vmem = pl.BlockSpec(memory_space=pltpu.VMEM)
    return pl.pallas_call(
        times_plane,
        out_shape=jax.ShapeDtypeStruct((rows, others), jnp.float32),
        in_specs=[vmem, vmem],
        out_specs=vmem,
        compiler_params=pltpu.CompilerParams(
            vmem_limit_bytes=4 * rows * others + 2 * (rows + others) * width + VMEM_SPARE
        ),
        cost_estimate=cost_of(rows, width, others),
    )(moving, plane)


def maxima_kernel(partners, count, two_sided, device, everyone, moving, plane, *refs):
    tiles = 1 + len(two_sided)
    given = dict(zip([0, *range(2, tiles)], refs))
    row_outs = refs[len(given) : len(given) + count]
    column_outs = list(refs[len(given) + count : -2])
    fresh, column_best = refs[-2:]
    rows = moving.shape[0]
    strip = min(STRIP, rows)
    per_block = rows // LANES
    chunk = fresh.shape[2]
    per_chunk = chunk // LANES
    chunks = plane.shape[0] // chunk
    shards = everyone.shape[0]
    words = -(-shards // WORD)
    source = device[...]
    table = pair_words(everyone[:, 2 * rows :], source, partners, words)

    def scale_of(at):
        return everyone[at : at + 1, 0:rows]

    def cluster_of(at):
        return everyone[at : at + 1, rows : 2 * rows].astype(jnp.int32)

    def bits_of(at):
        named = cluster_of(at) == source
        return [jnp.sum(jnp.where(named, t, 0.0), axis=0, keepdims=True).astype(jnp.int32) for t in table]

    def ones_of(at):
        named = cluster_of(at)
        return [jnp.where(named // WORD == w, jnp.int32(1) << (named % WORD), 0) for w in range(words)]

    def along_sublanes(value):
        return jnp.transpose(jnp.broadcast_to(value, (LANES, rows)))

    lane_scale = [scale_of(j) for j in range(count)]
    lane_ones = [ones_of(j) for j in range(count)]
    scale_down = [along_sublanes(scale_of(r * count)) for r in range(tiles)]
    bits_down = [[along_sublanes(b) for b in bits_of(r * count)] for r in range(tiles)]

    def lanes_of(per, g):
        first = g % per_block * LANES
        return per[g // per_block][:, first : first + LANES]

    row_part = {}

    def passed(r, c):
        wants_row = r > 0
        wants_column = r == 0 or two_sided[r - 1]
        for first in range(0, rows, strip):
            here = slice(first, first + strip)
            best = None
            for at in range(per_chunk):
                g = c * per_chunk + at
                if r in given:
                    value = given[r][here, g * LANES : (g + 1) * LANES]
                else:
                    value = fresh[c % 2, here, at * LANES : (at + 1) * LANES]
                met = bits_down[r][0][here] & lanes_of([o[0] for o in lane_ones], g)
                for w in range(1, words):
                    met = met | (bits_down[r][w][here] & lanes_of([o[w] for o in lane_ones], g))
                keep = met != 0
                if r == 0 and g < per_block and g * LANES < first + strip and first < (g + 1) * LANES:
                    down = lax.broadcasted_iota(jnp.int32, value.shape, 0) + first
                    across = lax.broadcasted_iota(jnp.int32, value.shape, 1) + g * LANES
                    keep = keep & (down != across)
                if wants_row:
                    value = jnp.where(keep, value * scale_down[r][here], LOWEST)
                    part = jnp.max(value.reshape(strip // SUBLANES, SUBLANES, LANES), axis=0)
                    row_part[g] = jnp.maximum(row_part[g], part) if g in row_part else part
                    if wants_column:
                        value = value * lanes_of(lane_scale, g)
                else:
                    value = jnp.where(keep, value * lanes_of(lane_scale, g), LOWEST)
                if wants_column:
                    best = value if best is None else jnp.maximum(best, value)
            if wants_column:
                column_best[r, here, :] = best if c == 0 else jnp.maximum(column_best[r, here, :], best)

    for c in range(chunks + 1):
        if c < chunks:
            fresh[c % 2] = lax.dot_general(
                moving[...],
                plane[c * chunk : (c + 1) * chunk, :],
                (((1,), (1,)), ((), ())),
                preferred_element_type=jnp.float32,
            )
            for r in given:
                passed(r, c)
        if c > 0:
            passed(1, c - 1)

    def column_of(r):
        return jnp.max(jnp.transpose(column_best[r]), axis=0, keepdims=True)

    for r in range(1, tiles):
        if two_sided[r - 1]:
            column_outs.pop(0)[...] = column_of(r)
    own_best = column_of(0) * scale_of(0)
    for j in range(count):
        for at in range(per_block):
            here = slice(at * LANES, (at + 1) * LANES)
            found = jnp.max(row_part[j * per_block + at], axis=0, keepdims=True) * lane_scale[j][:, here]
            if j == 0:
                found = jnp.maximum(found, own_best[:, here])
            row_outs[j][:, here] = found


def maxima(device, everyone, partners, moving, plane, given, two_sided):
    rows, width = moving.shape
    count = plane.shape[0] // rows
    chunk = min(256, rows)
    vmem = pl.BlockSpec(memory_space=pltpu.VMEM)
    outs = count + sum(two_sided)
    return pl.pallas_call(
        functools.partial(maxima_kernel, partners, count, tuple(two_sided)),
        out_shape=[jax.ShapeDtypeStruct((1, rows), jnp.float32)] * outs,
        in_specs=[vmem] * (4 + len(given)),
        out_specs=[vmem] * outs,
        scratch_shapes=[
            pltpu.VMEM((2, rows, chunk), jnp.float32),
            pltpu.VMEM((1 + len(two_sided), rows, LANES), jnp.float32),
        ],
        compiler_params=pltpu.CompilerParams(
            vmem_limit_bytes=4 * rows * plane.shape[0] * len(given)
            + 2 * width * (plane.shape[0] + rows)
            + 2 * VMEM_SPARE
        ),
        cost_estimate=cost_of(rows, width, plane.shape[0]),
    )(device, everyone, moving, plane, *given)


def pair_words(listed, source, partners, words):
    shards = listed.shape[0]
    lane = lax.broadcasted_iota(jnp.int32, listed.shape, 1)
    target = source + lane + 1
    used = (lane < partners) & (target < shards) & (listed == 1.0)

    def weight(which, w):
        return jnp.where(which // WORD == w, jnp.int32(1) << (which % WORD), 0).astype(jnp.float32)

    table = []
    for w in range(words):
        met = jnp.where(used, weight(target, w), 0.0) + jnp.where(lane == 0, weight(source, w), 0.0)
        met = jnp.sum(met, axis=1, keepdims=True)
        behind = jnp.where(used, weight(source, w), 0.0)
        for i in range(shards):
            hit = jnp.where(target == source[i : i + 1, :], behind, 0.0)
            here = jnp.sum(jnp.sum(hit, axis=0, keepdims=True), axis=1, keepdims=True)
            met = met + jnp.where(lax.broadcasted_iota(jnp.int32, met.shape, 0) == i, here, 0.0)
        table.append(met)
    return table


def joined_kernel(*refs):
    pieces, out = refs[:-2], refs[-1]
    at = 0
    for piece in pieces:
        out[at : at + piece.shape[0], :] = piece[...]
        at += piece.shape[0]


def joined(pieces, after):
    vmem = pl.BlockSpec(memory_space=pltpu.VMEM)
    return pl.pallas_call(
        joined_kernel,
        out_shape=jax.ShapeDtypeStruct((sum(p.shape[0] for p in pieces), pieces[0].shape[1]), jnp.float32),
        in_specs=[vmem] * len(pieces) + [pl.BlockSpec(memory_space=pl.ANY)],
        out_specs=vmem,
        compiler_params=pltpu.CompilerParams(vmem_limit_bytes=2**20),
    )(*pieces, after)


def device_table(shards, plane, planes, order, place_of, here):
    rel = jnp.arange(shards, dtype=jnp.int32)
    place = jnp.sum(jnp.where(jnp.arange(planes) == here // plane, jnp.asarray(place_of, jnp.int32), 0))
    place = (place - rel // plane) % planes
    z = jnp.sum(jnp.where(place[:, None] == jnp.arange(planes)[None, :], jnp.asarray(order, jnp.int32)[None, :], 0), axis=1)
    return (z * plane + (here % plane ^ rel % plane)).reshape(shards, 1)


def per_device(embeddings, scales, cluster, pair_listed):
    rows, width = embeddings.shape
    shards = lax.axis_size("shard")
    here = lax.axis_index("shard")
    plane = 1
    while plane * plane * 4 <= shards:
        plane *= 2
    planes = shards // plane
    half = planes // 2
    owned, partners = pair_listed.shape

    order = [place // 2 + (place % 2) * half for place in range(planes)]
    place_of = [order.index(z) for z in range(planes)]

    def permuted(value, target):
        return lax.ppermute(value, "shard", [(s, target(s)) for s in range(shards)])

    def across(bit):
        return lambda s: s ^ bit

    def along(distance):
        def target(s):
            z = order[(place_of[s // plane] + distance) % planes]
            return z * plane + s % plane

        return target

    arrived = {}
    for distance in range(1, half + 1):
        arrived[distance] = permuted(embeddings, along(distance))
    held = {0: embeddings}
    bit = plane // 2
    while bit:
        for j in sorted(held):
            held[j | bit] = permuted(held[j], across(bit))
        bit //= 2
    blocks = [held[j] for j in range(plane)]

    pairs = jnp.pad(pair_listed.reshape(-1).astype(jnp.float32), (0, -(owned * partners) % LANES))
    told = jnp.concatenate([scales.astype(jnp.float32), cluster[:, 0].astype(jnp.float32), pairs])[None, :]
    pieces, bit = [told], 1
    while bit < plane:
        mine = pieces[0] if len(pieces) == 1 else jnp.concatenate(pieces, axis=0)
        pieces.append(permuted(mine, across(bit)))
        bit *= 2
    raw, whole = gathered_plane(blocks)
    told = joined(pieces, raw)
    everyone = jnp.concatenate([told] + [permuted(told, along(t)) for t in range(1, planes)], axis=0)
    device = device_table(shards, plane, planes, order, place_of, here)
    distances = range(1, half + 1)
    two_sided = [2 * distance != planes for distance in distances]
    given = [raw] + [products(arrived[distance], whole) for distance in distances[1:]]
    found = maxima(device, everyone, partners, arrived[1], whole, given, two_sided)
    gathered, columns = found[:plane], list(found[plane:])

    result = gathered[0]
    returned = []
    for distance in distances:
        if two_sided[distance - 1]:
            returned.append(permuted(columns.pop(0), along(-distance)))
    returned += [permuted(gathered[j], across(j)) for j in range(plane - 1, 0, -1)]
    return functools.reduce(jnp.maximum, returned, result).reshape(rows)


def solution(mesh):
    placed = (
        P(("groups", "shard"), None),
        P(("groups", "shard")),
        P(("groups", "shard"), None),
        P(("groups", "shard"), None),
    )
    return jax.shard_map(
        per_device, mesh=mesh, in_specs=placed, out_specs=P(("groups", "shard")), check_vma=False
    )
```

```python
import functools

import jax
import jax.numpy as jnp
from jax import lax
from jax.experimental import pallas as pl
from jax.experimental.pallas import tpu as pltpu
from jax.sharding import PartitionSpec as P

LOWEST = float("-inf")
WORD = 16
LANES = 128
SUBLANES = 8
STRIP = 64
VMEM_SPARE = 4 * 2**20


def gather_kernel(count, *refs):
    blocks, out, plane, arrived = refs[:count], refs[count], refs[count + 1], refs[count + 2]
    rows = blocks[0].shape[0]
    copies = [
        pltpu.make_async_copy(block, plane.at[j * rows : (j + 1) * rows, :], arrived.at[j])
        for j, block in enumerate(blocks)
    ]
    for copy in copies:
        copy.start()
    for copy in copies:
        copy.wait()
    chunk = min(256, rows)
    for first in range(0, plane.shape[0], chunk):
        out[first : first + chunk, :] = lax.dot_general(
            plane[first : first + chunk, :],
            plane[:rows, :],
            (((1,), (1,)), ((), ())),
            preferred_element_type=jnp.float32,
        )


def product_kernel(moving, plane, after, out):
    chunk = min(256, moving.shape[0])
    for first in range(0, plane.shape[0], chunk):
        out[:, first : first + chunk] = lax.dot_general(
            moving[...],
            plane[first : first + chunk, :],
            (((1,), (1,)), ((), ())),
            preferred_element_type=jnp.float32,
        )


def cost_of(rows, width, others):
    return pl.CostEstimate(
        flops=2 * rows * others * width, bytes_accessed=2 * (rows + others) * width, transcendentals=0
    )


def gathered_plane(blocks):
    rows, width = blocks[0].shape
    others = rows * len(blocks)
    vmem = pl.BlockSpec(memory_space=pltpu.VMEM)
    return pl.pallas_call(
        functools.partial(gather_kernel, len(blocks)),
        out_shape=[
            jax.ShapeDtypeStruct((others, rows), jnp.float32),
            jax.ShapeDtypeStruct((others, width), blocks[0].dtype),
        ],
        in_specs=[pl.BlockSpec(memory_space=pl.ANY)] * len(blocks),
        out_specs=[vmem, vmem],
        scratch_shapes=[pltpu.SemaphoreType.DMA((len(blocks),))],
        compiler_params=pltpu.CompilerParams(vmem_limit_bytes=4 * rows * others + 2 * others * width + VMEM_SPARE),
        cost_estimate=cost_of(rows, width, others),
    )(*blocks)


def products(moving, plane, after):
    rows, width = moving.shape
    others = plane.shape[0]
    vmem = pl.BlockSpec(memory_space=pltpu.VMEM)
    return pl.pallas_call(
        product_kernel,
        out_shape=jax.ShapeDtypeStruct((rows, others), jnp.float32),
        in_specs=[vmem, vmem, pl.BlockSpec(memory_space=pl.ANY)],
        out_specs=vmem,
        compiler_params=pltpu.CompilerParams(
            vmem_limit_bytes=4 * rows * others + 2 * (rows + others) * width + VMEM_SPARE
        ),
        cost_estimate=cost_of(rows, width, others),
    )(moving, plane, after)


def along_sublanes(value):
    return jnp.transpose(jnp.broadcast_to(value, (LANES, value.shape[1])))


def classes_kernel(told, raw, out, scale_down, cluster_down):
    count, rows = told.shape[0], raw.shape[1]
    strip = min(STRIP, rows)
    for j in range(count):
        here = slice(j * rows, (j + 1) * rows)
        scale_down[here, :] = along_sublanes(told[j : j + 1, 0:rows])
        cluster_down[here, :] = along_sublanes(told[j : j + 1, rows : 2 * rows])
    subclusters = out.shape[0]
    for first in range(0, rows, LANES):

        def step(i, best):
            here = pl.ds(pl.multiple_of(i * strip, strip), strip)
            down = lax.broadcasted_iota(jnp.int32, (strip, LANES), 0) + i * strip
            across = lax.broadcasted_iota(jnp.int32, (strip, LANES), 1) + first
            value = raw[here, first : first + LANES] * scale_down[here, :]
            value = jnp.where(down == across, LOWEST, value)
            cluster = cluster_down[here, :]
            found = []
            for a in range(subclusters):
                one = jnp.where(cluster == float(a), value, LOWEST)
                one = jnp.max(one.reshape(strip // SUBLANES, SUBLANES, LANES), axis=0)
                found.append(jnp.maximum(best[a], one))
            return tuple(found)

        start = tuple(jnp.full((SUBLANES, LANES), LOWEST, jnp.float32) for _ in range(subclusters))
        best = lax.fori_loop(0, raw.shape[0] // strip, step, start)
        for a in range(subclusters):
            out[a : a + 1, first : first + LANES] = jnp.max(best[a], axis=0, keepdims=True)


def classes(told, raw, subclusters):
    others, rows = raw.shape
    vmem = pl.BlockSpec(memory_space=pltpu.VMEM)
    return pl.pallas_call(
        classes_kernel,
        out_shape=jax.ShapeDtypeStruct((subclusters, rows), jnp.float32),
        in_specs=[vmem, vmem],
        out_specs=vmem,
        scratch_shapes=[pltpu.VMEM((others, LANES), jnp.float32)] * 2,
        compiler_params=pltpu.CompilerParams(vmem_limit_bytes=4 * others * (rows + 2 * LANES) + VMEM_SPARE),
    )(told, raw)


def maxima_kernel(partners, count, others, two_sided, device, told, own_classes, moving, plane, *refs):
    tiles = 1 + len(two_sided)
    distant, refs = refs[:others], refs[others:]
    given = dict(zip(range(2, tiles), refs))
    row_outs = refs[len(given) : len(given) + count]
    column_outs = list(refs[len(given) + count : -2])
    fresh, column_best = refs[-2:]
    rows = moving.shape[0]
    strip = min(STRIP, rows)
    per_block = rows // LANES
    chunk = fresh.shape[2]
    per_chunk = chunk // LANES
    chunks = plane.shape[0] // chunk
    shards = device.shape[0]
    words = -(-shards // WORD)
    source = device[...]
    pairs = [told[:, 2 * rows :]] + [d[0:count, 2 * LANES :] for d in distant]
    table = pair_words(jnp.concatenate(pairs, axis=0), source, partners, words)

    def facts_of(r):
        if r == 0:
            return told[0:1, 0:rows], told[0:1, rows : 2 * rows]
        parts = [distant[r - 1][p : p + 1, 0 : 2 * LANES] for p in range(rows // LANES)]
        return [jnp.concatenate([p[:, at : at + LANES] for p in parts], axis=1) for at in (0, LANES)]

    def bits_of(clusters):
        named = clusters.astype(jnp.int32) == source
        return [jnp.sum(jnp.where(named, t, 0.0), axis=0, keepdims=True).astype(jnp.int32) for t in table]

    def ones_of(at):
        named = told[at : at + 1, rows : 2 * rows].astype(jnp.int32)
        return [jnp.where(named // WORD == w, jnp.int32(1) << (named % WORD), 0) for w in range(words)]

    lane_scale = [told[j : j + 1, 0:rows] for j in range(count)]
    lane_ones = [ones_of(j) for j in range(count)]
    facts = [facts_of(r) for r in range(tiles)]
    scale_down = {r: along_sublanes(facts[r][0]) for r in range(1, tiles)}
    bits_down = {r: [along_sublanes(b) for b in bits_of(facts[r][1])] for r in range(1, tiles)}

    def lanes_of(per, g):
        first = g % per_block * LANES
        return per[g // per_block][:, first : first + LANES]

    row_part = {}

    def passed(r, c):
        wants_column = two_sided[r - 1]
        for first in range(0, rows, strip):
            here = slice(first, first + strip)
            best = None
            for at in range(per_chunk):
                g = c * per_chunk + at
                if r in given:
                    value = given[r][here, g * LANES : (g + 1) * LANES]
                else:
                    value = fresh[c % 2, here, at * LANES : (at + 1) * LANES]
                met = bits_down[r][0][here] & lanes_of([o[0] for o in lane_ones], g)
                for w in range(1, words):
                    met = met | (bits_down[r][w][here] & lanes_of([o[w] for o in lane_ones], g))
                keep = met != 0
                value = jnp.where(keep, value * scale_down[r][here], LOWEST)
                part = jnp.max(value.reshape(strip // SUBLANES, SUBLANES, LANES), axis=0)
                row_part[g] = jnp.maximum(row_part[g], part) if g in row_part else part
                if wants_column:
                    value = value * lanes_of(lane_scale, g)
                if wants_column:
                    best = value if best is None else jnp.maximum(best, value)
            if wants_column:
                column_best[r, here, :] = best if c == 0 else jnp.maximum(column_best[r, here, :], best)

    for c in range(chunks + 1):
        if c < chunks:
            fresh[c % 2] = lax.dot_general(
                moving[...],
                plane[c * chunk : (c + 1) * chunk, :],
                (((1,), (1,)), ((), ())),
                preferred_element_type=jnp.float32,
            )
            for r in given:
                passed(r, c)
        if c > 0:
            passed(1, c - 1)

    def column_of(r):
        return jnp.max(jnp.transpose(column_best[r]), axis=0, keepdims=True)

    for r in range(1, tiles):
        if two_sided[r - 1]:
            column_outs.pop(0)[...] = column_of(r)
    own_bits = bits_of(facts[0][1])
    own_best = jnp.full((1, rows), LOWEST, jnp.float32)
    for w in range(words):
        first = w * WORD
        part = own_classes[first : min(first + WORD, shards), :]
        bit = jnp.int32(1) << lax.broadcasted_iota(jnp.int32, part.shape, 0)
        part = jnp.where((own_bits[w] & bit) != 0, part, LOWEST)
        own_best = jnp.maximum(own_best, jnp.max(part, axis=0, keepdims=True))
    own_best = own_best * lane_scale[0]
    for j in range(count):
        for at in range(per_block):
            here = slice(at * LANES, (at + 1) * LANES)
            found = jnp.max(row_part[j * per_block + at], axis=0, keepdims=True) * lane_scale[j][:, here]
            if j == 0:
                found = jnp.maximum(found, own_best[:, here])
            row_outs[j][:, here] = found


def maxima(device, told, own_classes, distant, partners, moving, plane, given, two_sided):
    rows, width = moving.shape
    count = plane.shape[0] // rows
    chunk = min(256, rows)
    vmem = pl.BlockSpec(memory_space=pltpu.VMEM)
    outs = count + sum(two_sided)
    return pl.pallas_call(
        functools.partial(maxima_kernel, partners, count, len(distant), tuple(two_sided)),
        out_shape=[jax.ShapeDtypeStruct((1, rows), jnp.float32)] * outs,
        in_specs=[vmem] * (5 + len(distant) + len(given)),
        out_specs=[vmem] * outs,
        scratch_shapes=[
            pltpu.VMEM((2, rows, chunk), jnp.float32),
            pltpu.VMEM((1 + len(two_sided), rows, LANES), jnp.float32),
        ],
        compiler_params=pltpu.CompilerParams(
            vmem_limit_bytes=4 * rows * plane.shape[0] * len(given)
            + 2 * width * (plane.shape[0] + rows)
            + 2 * VMEM_SPARE
        ),
        cost_estimate=cost_of(rows, width, plane.shape[0]),
    )(device, told, own_classes, moving, plane, *distant, *given)


def pair_words(listed, source, partners, words):
    shards = listed.shape[0]
    lane = lax.broadcasted_iota(jnp.int32, listed.shape, 1)
    target = source + lane + 1
    used = (lane < partners) & (target < shards) & (listed == 1.0)

    def weight(which, w):
        return jnp.where(which // WORD == w, jnp.int32(1) << (which % WORD), 0).astype(jnp.float32)

    table = []
    for w in range(words):
        met = jnp.where(used, weight(target, w), 0.0) + jnp.where(lane == 0, weight(source, w), 0.0)
        met = jnp.sum(met, axis=1, keepdims=True)
        behind = jnp.where(used, weight(source, w), 0.0)
        for i in range(shards):
            hit = jnp.where(target == source[i : i + 1, :], behind, 0.0)
            here = jnp.sum(jnp.sum(hit, axis=0, keepdims=True), axis=1, keepdims=True)
            met = met + jnp.where(lax.broadcasted_iota(jnp.int32, met.shape, 0) == i, here, 0.0)
        table.append(met)
    return table


def joined_kernel(plane, *refs):
    pieces, told, packed = refs[:-3], refs[-2], refs[-1]
    at = 0
    for piece in pieces:
        told[at : at + piece.shape[0], :] = piece[...]
        at += piece.shape[0]
    rows = packed.shape[1] - 2 * LANES
    facts = (pieces[0].shape[1] - rows) // 2
    packed[...] = jnp.zeros(packed.shape, packed.dtype)
    for part in range(facts // LANES):
        here = slice(part * LANES, (part + 1) * LANES)
        packed[part : part + 1, 0:LANES] = pieces[0][0:1, here]
        packed[part : part + 1, LANES : 2 * LANES] = pieces[0][0:1, facts + part * LANES : facts + (part + 1) * LANES]
    packed[0:plane, 2 * LANES :] = told[0:plane, 2 * facts :]


def joined(pieces, facts, after):
    vmem = pl.BlockSpec(memory_space=pltpu.VMEM)
    length = pieces[0].shape[1]
    plane = sum(p.shape[0] for p in pieces)
    return pl.pallas_call(
        functools.partial(joined_kernel, plane),
        out_shape=[
            jax.ShapeDtypeStruct((plane, length), jnp.float32),
            jax.ShapeDtypeStruct((max(plane, facts // LANES), length - 2 * facts + 2 * LANES), jnp.float32),
        ],
        in_specs=[vmem] * len(pieces) + [pl.BlockSpec(memory_space=pl.ANY)],
        out_specs=[vmem, vmem],
        compiler_params=pltpu.CompilerParams(vmem_limit_bytes=2**20),
    )(*pieces, after)


def device_table(shards, plane, planes, order, place_of, here):
    rel = jnp.arange(shards, dtype=jnp.int32)
    place = jnp.sum(jnp.where(jnp.arange(planes) == here // plane, jnp.asarray(place_of, jnp.int32), 0))
    place = (place - rel // plane) % planes
    z = jnp.sum(jnp.where(place[:, None] == jnp.arange(planes)[None, :], jnp.asarray(order, jnp.int32)[None, :], 0), axis=1)
    return (z * plane + (here % plane ^ rel % plane)).reshape(shards, 1)


def per_device(embeddings, scales, cluster, pair_listed):
    rows, width = embeddings.shape
    shards = lax.axis_size("shard")
    here = lax.axis_index("shard")
    plane = 1
    while plane * plane * 4 <= shards:
        plane *= 2
    planes = shards // plane
    half = planes // 2
    owned, partners = pair_listed.shape

    order = [place // 2 + (place % 2) * half for place in range(planes)]
    place_of = [order.index(z) for z in range(planes)]

    def permuted(value, target):
        return lax.ppermute(value, "shard", [(s, target(s)) for s in range(shards)])

    def across(bit):
        return lambda s: s ^ bit

    def along(distance):
        def target(s):
            z = order[(place_of[s // plane] + distance) % planes]
            return z * plane + s % plane

        return target

    arrived = {}
    for distance in range(1, half + 1):
        arrived[distance] = permuted(embeddings, along(distance))
    held = {0: embeddings}
    bit = plane // 2
    while bit:
        for j in sorted(held):
            held[j | bit] = permuted(held[j], across(bit))
        bit //= 2
    blocks = [held[j] for j in range(plane)]

    pairs = jnp.pad(pair_listed.reshape(-1).astype(jnp.float32), (0, -(owned * partners) % LANES))
    told = jnp.concatenate([scales.astype(jnp.float32), cluster[:, 0].astype(jnp.float32), pairs])[None, :]
    pieces, bit = [told], 1
    while bit < plane:
        mine = pieces[0] if len(pieces) == 1 else jnp.concatenate(pieces, axis=0)
        pieces.append(permuted(mine, across(bit)))
        bit *= 2
    raw, whole = gathered_plane(blocks)
    told, packed = joined(pieces, rows, raw)
    distant = [permuted(packed, along(t)) for t in range(1, planes)]
    device = device_table(shards, plane, planes, order, place_of, here)
    distances = range(1, half + 1)
    two_sided = [2 * distance != planes for distance in distances]
    own_classes = classes(told, raw, shards)
    given = [products(arrived[distance], whole, own_classes) for distance in distances[1:]]
    found = maxima(device, told, own_classes, distant, partners, arrived[1], whole, given, two_sided)
    gathered, columns = found[:plane], list(found[plane:])

    result = gathered[0]
    returned = []
    for distance in distances:
        if two_sided[distance - 1]:
            returned.append(permuted(columns.pop(0), along(-distance)))
    returned += [permuted(gathered[j], across(j)) for j in range(plane - 1, 0, -1)]
    return functools.reduce(jnp.maximum, returned, result).reshape(rows)


def solution(mesh):
    placed = (
        P(("groups", "shard"), None),
        P(("groups", "shard")),
        P(("groups", "shard"), None),
        P(("groups", "shard"), None),
    )
    return jax.shard_map(
        per_device, mesh=mesh, in_specs=placed, out_specs=P(("groups", "shard")), check_vma=False
    )
```

```python
import functools

import jax
import jax.numpy as jnp
from jax import lax
from jax.experimental import pallas as pl
from jax.experimental.pallas import tpu as pltpu
from jax.sharding import PartitionSpec as P

LOWEST = float("-inf")
WORD = 16
LANES = 128
SUBLANES = 8
STRIP = 64
VMEM_SPARE = 4 * 2**20


def gather_kernel(count, *refs):
    blocks, out, plane, arrived = refs[:count], refs[count], refs[count + 1], refs[count + 2]
    rows = blocks[0].shape[0]
    copies, at = [], 0
    for j, block in enumerate(blocks):
        copies.append(pltpu.make_async_copy(block, plane.at[at : at + block.shape[0], :], arrived.at[j]))
        at += block.shape[0]
    for copy in copies:
        copy.start()
    at = 0
    for copy, block in zip(copies, blocks):
        copy.wait()
        chunk = min(256, block.shape[0])
        for first in range(at, at + block.shape[0], chunk):
            out[first : first + chunk, :] = lax.dot_general(
                plane[first : first + chunk, :],
                plane[:rows, :],
                (((1,), (1,)), ((), ())),
                preferred_element_type=jnp.float32,
            )
        at += block.shape[0]


def product_kernel(moving, plane, after, out):
    chunk = min(256, moving.shape[0])
    for first in range(0, plane.shape[0], chunk):
        out[:, first : first + chunk] = lax.dot_general(
            moving[...],
            plane[first : first + chunk, :],
            (((1,), (1,)), ((), ())),
            preferred_element_type=jnp.float32,
        )


def cost_of(rows, width, others):
    return pl.CostEstimate(
        flops=2 * rows * others * width, bytes_accessed=2 * (rows + others) * width, transcendentals=0
    )


def gathered_plane(blocks):
    rows, width = blocks[0].shape
    others = sum(block.shape[0] for block in blocks)
    vmem = pl.BlockSpec(memory_space=pltpu.VMEM)
    return pl.pallas_call(
        functools.partial(gather_kernel, len(blocks)),
        out_shape=[
            jax.ShapeDtypeStruct((others, rows), jnp.float32),
            jax.ShapeDtypeStruct((others, width), blocks[0].dtype),
        ],
        in_specs=[pl.BlockSpec(memory_space=pl.ANY)] * len(blocks),
        out_specs=[vmem, vmem],
        scratch_shapes=[pltpu.SemaphoreType.DMA((len(blocks),))],
        compiler_params=pltpu.CompilerParams(vmem_limit_bytes=4 * rows * others + 2 * others * width + VMEM_SPARE),
        cost_estimate=cost_of(rows, width, others),
    )(*blocks)


def products(moving, plane, after):
    rows, width = moving.shape
    others = plane.shape[0]
    vmem = pl.BlockSpec(memory_space=pltpu.VMEM)
    return pl.pallas_call(
        product_kernel,
        out_shape=jax.ShapeDtypeStruct((rows, others), jnp.float32),
        in_specs=[vmem, vmem, pl.BlockSpec(memory_space=pl.ANY)],
        out_specs=vmem,
        compiler_params=pltpu.CompilerParams(
            vmem_limit_bytes=4 * rows * others + 2 * (rows + others) * width + VMEM_SPARE
        ),
        cost_estimate=cost_of(rows, width, others),
    )(moving, plane, after)


def along_sublanes(value):
    return jnp.transpose(jnp.broadcast_to(value, (LANES, value.shape[1])))


def classes_kernel(partners, told, raw, out, scale_down, cluster_down):
    count, rows = told.shape[0], raw.shape[1]
    strip = min(STRIP, rows)
    for j in range(count):
        here = slice(j * rows, (j + 1) * rows)
        scale_down[here, :] = along_sublanes(told[j : j + 1, 0:rows])
        cluster_down[here, :] = along_sublanes(told[j : j + 1, rows : 2 * rows])
    offsets = range(-partners, partners + 1)
    for first in range(0, rows, LANES):
        mine = told[0:1, rows + first : rows + first + LANES]

        def step(i, best):
            here = pl.ds(pl.multiple_of(i * strip, strip), strip)
            down = lax.broadcasted_iota(jnp.int32, (strip, LANES), 0) + i * strip
            across = lax.broadcasted_iota(jnp.int32, (strip, LANES), 1) + first
            value = raw[here, first : first + LANES] * scale_down[here, :]
            value = jnp.where(down == across, LOWEST, value)
            ahead = cluster_down[here, :] - mine
            found = []
            for before, offset in zip(best, offsets):
                one = jnp.where(ahead == float(offset), value, LOWEST)
                one = jnp.max(one.reshape(strip // SUBLANES, SUBLANES, LANES), axis=0)
                found.append(jnp.maximum(before, one))
            return tuple(found)

        start = tuple(jnp.full((SUBLANES, LANES), LOWEST, jnp.float32) for _ in offsets)
        best = lax.fori_loop(0, raw.shape[0] // strip, step, start)
        for k, one in enumerate(best):
            out[k : k + 1, first : first + LANES] = jnp.max(one, axis=0, keepdims=True)


def classes(told, raw, partners):
    others, rows = raw.shape
    vmem = pl.BlockSpec(memory_space=pltpu.VMEM)
    return pl.pallas_call(
        functools.partial(classes_kernel, partners),
        out_shape=jax.ShapeDtypeStruct((2 * partners + 1, rows), jnp.float32),
        in_specs=[vmem, vmem],
        out_specs=vmem,
        scratch_shapes=[pltpu.VMEM((others, LANES), jnp.float32)] * 2,
        compiler_params=pltpu.CompilerParams(vmem_limit_bytes=4 * others * (rows + 2 * LANES) + VMEM_SPARE),
    )(told, raw)


def maxima_kernel(partners, count, others, two_sided, device, told, own_classes, moving, plane, *refs):
    tiles = 1 + len(two_sided)
    distant, refs = refs[:others], refs[others:]
    given = dict(zip(range(2, tiles), refs))
    row_outs = refs[len(given) : len(given) + count]
    column_outs = list(refs[len(given) + count : -2])
    fresh, column_best = refs[-2:]
    rows = moving.shape[0]
    strip = min(STRIP, rows)
    per_block = rows // LANES
    chunk = fresh.shape[2]
    per_chunk = chunk // LANES
    chunks = plane.shape[0] // chunk
    shards = device.shape[0]
    words = -(-shards // WORD)
    source = device[...]
    pairs = [told[:, 2 * rows :]] + [d[0:count, 2 * LANES :] for d in distant]
    table = pair_words(jnp.concatenate(pairs, axis=0), source, partners, words)

    def facts_of(r):
        if r == 0:
            return told[0:1, 0:rows], told[0:1, rows : 2 * rows]
        parts = [distant[r - 1][p : p + 1, 0 : 2 * LANES] for p in range(rows // LANES)]
        return [jnp.concatenate([p[:, at : at + LANES] for p in parts], axis=1) for at in (0, LANES)]

    def bits_of(clusters):
        named = clusters.astype(jnp.int32) == source
        return [jnp.sum(jnp.where(named, t, 0.0), axis=0, keepdims=True).astype(jnp.int32) for t in table]

    def ones_of(at):
        named = told[at : at + 1, rows : 2 * rows].astype(jnp.int32)
        return [jnp.where(named // WORD == w, jnp.int32(1) << (named % WORD), 0) for w in range(words)]

    lane_scale = [told[j : j + 1, 0:rows] for j in range(count)]
    lane_ones = [ones_of(j) for j in range(count)]
    facts = [facts_of(r) for r in range(tiles)]
    scale_down = {r: along_sublanes(facts[r][0]) for r in range(1, tiles)}
    bits_down = {r: [along_sublanes(b) for b in bits_of(facts[r][1])] for r in range(1, tiles)}

    def lanes_of(per, g):
        first = g % per_block * LANES
        return per[g // per_block][:, first : first + LANES]

    row_part = {}

    def passed(r, c):
        wants_column = two_sided[r - 1]
        for first in range(0, rows, strip):
            here = slice(first, first + strip)
            best = None
            for at in range(per_chunk):
                g = c * per_chunk + at
                if r in given:
                    value = given[r][here, g * LANES : (g + 1) * LANES]
                else:
                    value = fresh[c % 2, here, at * LANES : (at + 1) * LANES]
                met = bits_down[r][0][here] & lanes_of([o[0] for o in lane_ones], g)
                for w in range(1, words):
                    met = met | (bits_down[r][w][here] & lanes_of([o[w] for o in lane_ones], g))
                keep = met != 0
                value = jnp.where(keep, value * scale_down[r][here], LOWEST)
                part = jnp.max(value.reshape(strip // SUBLANES, SUBLANES, LANES), axis=0)
                row_part[g] = jnp.maximum(row_part[g], part) if g in row_part else part
                if wants_column:
                    value = value * lanes_of(lane_scale, g)
                if wants_column:
                    best = value if best is None else jnp.maximum(best, value)
            if wants_column:
                column_best[r, here, :] = best if c == 0 else jnp.maximum(column_best[r, here, :], best)

    for c in range(chunks + 1):
        if c < chunks:
            fresh[c % 2] = lax.dot_general(
                moving[...],
                plane[c * chunk : (c + 1) * chunk, :],
                (((1,), (1,)), ((), ())),
                preferred_element_type=jnp.float32,
            )
            for r in given:
                passed(r, c)
        if c > 0:
            passed(1, c - 1)

    def column_of(r):
        return jnp.max(jnp.transpose(column_best[r]), axis=0, keepdims=True)

    for r in range(1, tiles):
        if two_sided[r - 1]:
            column_outs.pop(0)[...] = column_of(r)
    own_bits = bits_of(facts[0][1])
    own_best = jnp.full((1, rows), LOWEST, jnp.float32)
    named = facts[0][1].astype(jnp.int32)
    for k in range(2 * partners + 1):
        met = jnp.int32(0)
        other = named + (k - partners)
        for w in range(words):
            bit = jnp.where((other >= 0) & (other // WORD == w), jnp.int32(1) << (other % WORD), 0)
            met = met | (own_bits[w] & bit)
        own_best = jnp.maximum(own_best, jnp.where(met != 0, own_classes[k : k + 1, :], LOWEST))
    own_best = own_best * lane_scale[0]
    for j in range(count):
        for at in range(per_block):
            here = slice(at * LANES, (at + 1) * LANES)
            found = jnp.max(row_part[j * per_block + at], axis=0, keepdims=True) * lane_scale[j][:, here]
            if j == 0:
                found = jnp.maximum(found, own_best[:, here])
            row_outs[j][:, here] = found


def maxima(device, told, own_classes, distant, partners, moving, plane, given, two_sided):
    rows, width = moving.shape
    count = plane.shape[0] // rows
    chunk = min(256, rows)
    vmem = pl.BlockSpec(memory_space=pltpu.VMEM)
    outs = count + sum(two_sided)
    return pl.pallas_call(
        functools.partial(maxima_kernel, partners, count, len(distant), tuple(two_sided)),
        out_shape=[jax.ShapeDtypeStruct((1, rows), jnp.float32)] * outs,
        in_specs=[vmem] * (5 + len(distant) + len(given)),
        out_specs=[vmem] * outs,
        scratch_shapes=[
            pltpu.VMEM((2, rows, chunk), jnp.float32),
            pltpu.VMEM((1 + len(two_sided), rows, LANES), jnp.float32),
        ],
        compiler_params=pltpu.CompilerParams(
            vmem_limit_bytes=4 * rows * plane.shape[0] * len(given)
            + 2 * width * (plane.shape[0] + rows)
            + 2 * VMEM_SPARE
        ),
        cost_estimate=cost_of(rows, width, plane.shape[0]),
    )(device, told, own_classes, moving, plane, *distant, *given)


def pair_words(listed, source, partners, words):
    shards = listed.shape[0]
    lane = lax.broadcasted_iota(jnp.int32, listed.shape, 1)
    target = source + lane + 1
    used = (lane < partners) & (target < shards) & (listed == 1.0)

    def weight(which, w):
        return jnp.where(which // WORD == w, jnp.int32(1) << (which % WORD), 0).astype(jnp.float32)

    table = []
    for w in range(words):
        met = jnp.where(used, weight(target, w), 0.0) + jnp.where(lane == 0, weight(source, w), 0.0)
        met = jnp.sum(met, axis=1, keepdims=True)
        behind = jnp.where(used, weight(source, w), 0.0)
        for i in range(shards):
            hit = jnp.where(target == source[i : i + 1, :], behind, 0.0)
            here = jnp.sum(jnp.sum(hit, axis=0, keepdims=True), axis=1, keepdims=True)
            met = met + jnp.where(lax.broadcasted_iota(jnp.int32, met.shape, 0) == i, here, 0.0)
        table.append(met)
    return table


def kept_kernel(value, after, out):
    out[...] = value[...]


def kept(value, after):
    vmem = pl.BlockSpec(memory_space=pltpu.VMEM)
    return pl.pallas_call(
        kept_kernel,
        out_shape=jax.ShapeDtypeStruct(value.shape, value.dtype),
        in_specs=[vmem, pl.BlockSpec(memory_space=pl.ANY)],
        out_specs=vmem,
        compiler_params=pltpu.CompilerParams(vmem_limit_bytes=2**20),
    )(value, after)


def joined_kernel(plane, *refs):
    pieces, told, packed = refs[:-3], refs[-2], refs[-1]
    at = 0
    for piece in pieces:
        told[at : at + piece.shape[0], :] = piece[...]
        at += piece.shape[0]
    rows = packed.shape[1] - 2 * LANES
    facts = (pieces[0].shape[1] - rows) // 2
    packed[...] = jnp.zeros(packed.shape, packed.dtype)
    for part in range(facts // LANES):
        here = slice(part * LANES, (part + 1) * LANES)
        packed[part : part + 1, 0:LANES] = pieces[0][0:1, here]
        packed[part : part + 1, LANES : 2 * LANES] = pieces[0][0:1, facts + part * LANES : facts + (part + 1) * LANES]
    packed[0:plane, 2 * LANES :] = told[0:plane, 2 * facts :]


def joined(pieces, facts, after):
    vmem = pl.BlockSpec(memory_space=pltpu.VMEM)
    length = pieces[0].shape[1]
    plane = sum(p.shape[0] for p in pieces)
    return pl.pallas_call(
        functools.partial(joined_kernel, plane),
        out_shape=[
            jax.ShapeDtypeStruct((plane, length), jnp.float32),
            jax.ShapeDtypeStruct((max(plane, facts // LANES), length - 2 * facts + 2 * LANES), jnp.float32),
        ],
        in_specs=[vmem] * len(pieces) + [pl.BlockSpec(memory_space=pl.ANY)],
        out_specs=[vmem, vmem],
        compiler_params=pltpu.CompilerParams(vmem_limit_bytes=2**20),
    )(*pieces, after)


def device_table(shards, plane, planes, order, place_of, here):
    rel = jnp.arange(shards, dtype=jnp.int32)
    place = jnp.sum(jnp.where(jnp.arange(planes) == here // plane, jnp.asarray(place_of, jnp.int32), 0))
    place = (place - rel // plane) % planes
    z = jnp.sum(jnp.where(place[:, None] == jnp.arange(planes)[None, :], jnp.asarray(order, jnp.int32)[None, :], 0), axis=1)
    return (z * plane + (here % plane ^ rel % plane)).reshape(shards, 1)


def per_device(embeddings, scales, cluster, pair_listed):
    rows, width = embeddings.shape
    shards = lax.axis_size("shard")
    here = lax.axis_index("shard")
    plane = 1
    while plane * plane * 4 <= shards:
        plane *= 2
    planes = shards // plane
    half = planes // 2
    owned, partners = pair_listed.shape

    order = [place // 2 + (place % 2) * half for place in range(planes)]
    place_of = [order.index(z) for z in range(planes)]

    def permuted(value, target):
        return lax.ppermute(value, "shard", [(s, target(s)) for s in range(shards)])

    def across(bit):
        return lambda s: s ^ bit

    def along(distance):
        def target(s):
            z = order[(place_of[s // plane] + distance) % planes]
            return z * plane + s % plane

        return target

    arrived = {}
    for distance in range(1, half + 1):
        arrived[distance] = permuted(embeddings, along(distance))
    parts = 2
    size = rows // parts
    held = {(0, p): embeddings[p * size : (p + 1) * size] for p in range(parts)}
    whole_block = {0: embeddings}
    bit = plane // 2
    while bit:
        for j, p in sorted(held):
            if bit == 1 and j == 0:
                continue
            held[j | bit, p] = permuted(held[j, p], across(bit))
        bit //= 2
    whole_block[1] = permuted(embeddings, across(1))
    blocks = []
    for j in range(plane):
        blocks += [whole_block[j]] if j in whole_block else [held[j, p] for p in range(parts)]

    pairs = jnp.pad(pair_listed.reshape(-1).astype(jnp.float32), (0, -(owned * partners) % LANES))
    told = jnp.concatenate([scales.astype(jnp.float32), cluster[:, 0].astype(jnp.float32), pairs])[None, :]
    told = kept(told, held[plane // 2, 0])
    pieces, bit = [told], 1
    while bit < plane:
        mine = pieces[0] if len(pieces) == 1 else jnp.concatenate(pieces, axis=0)
        pieces.append(permuted(mine, across(bit)))
        bit *= 2
    raw, whole = gathered_plane(blocks)
    told, packed = joined(pieces, rows, raw)
    distant = [permuted(packed, along(t)) for t in range(1, planes)]
    device = device_table(shards, plane, planes, order, place_of, here)
    distances = range(1, half + 1)
    two_sided = [2 * distance != planes for distance in distances]
    own_classes = classes(told, raw, partners)
    given = [products(arrived[distance], whole, own_classes) for distance in distances[1:]]
    found = maxima(device, told, own_classes, distant, partners, arrived[1], whole, given, two_sided)
    gathered, columns = found[:plane], list(found[plane:])

    result = gathered[0]
    returned = []
    for distance in distances:
        if two_sided[distance - 1]:
            returned.append(permuted(columns.pop(0), along(-distance)))
    returned += [permuted(gathered[j], across(j)) for j in range(plane - 1, 0, -1)]
    return functools.reduce(jnp.maximum, returned, result).reshape(rows)


def solution(mesh):
    placed = (
        P(("groups", "shard"), None),
        P(("groups", "shard")),
        P(("groups", "shard"), None),
        P(("groups", "shard"), None),
    )
    return jax.shard_map(
        per_device, mesh=mesh, in_specs=placed, out_specs=P(("groups", "shard")), check_vma=False
    )
```

```python
import functools

import jax
import jax.numpy as jnp
from jax import lax
from jax.experimental import pallas as pl
from jax.experimental.pallas import tpu as pltpu
from jax.sharding import PartitionSpec as P

LOWEST = float("-inf")
WORD = 16
LANES = 128
SUBLANES = 8
STRIP = 64
VMEM_SPARE = 4 * 2**20


def gather_kernel(count, *refs):
    blocks, out, plane, arrived = refs[:count], refs[count], refs[count + 1], refs[count + 2]
    rows = blocks[0].shape[0]
    copies, at = [], 0
    for j, block in enumerate(blocks):
        copies.append(pltpu.make_async_copy(block, plane.at[at : at + block.shape[0], :], arrived.at[j]))
        at += block.shape[0]
    for copy in copies:
        copy.start()
    for copy in copies:
        copy.wait()
    times_plane(plane.at[:rows, :], plane, out)


def times_plane(moving, plane, out):
    chunk = min(256, moving.shape[0])
    for first in range(0, plane.shape[0], chunk):
        out[:, first : first + chunk] = lax.dot_general(
            moving[...],
            plane[first : first + chunk, :],
            (((1,), (1,)), ((), ())),
            preferred_element_type=jnp.float32,
        )


def cost_of(rows, width, others):
    return pl.CostEstimate(
        flops=2 * rows * others * width, bytes_accessed=2 * (rows + others) * width, transcendentals=0
    )


def gathered_plane(blocks):
    rows, width = blocks[0].shape
    others = sum(block.shape[0] for block in blocks)
    vmem = pl.BlockSpec(memory_space=pltpu.VMEM)
    return pl.pallas_call(
        functools.partial(gather_kernel, len(blocks)),
        out_shape=[
            jax.ShapeDtypeStruct((rows, others), jnp.float32),
            jax.ShapeDtypeStruct((others, width), blocks[0].dtype),
        ],
        in_specs=[pl.BlockSpec(memory_space=pl.ANY)] * len(blocks),
        out_specs=[vmem, vmem],
        scratch_shapes=[pltpu.SemaphoreType.DMA((len(blocks),))],
        compiler_params=pltpu.CompilerParams(vmem_limit_bytes=4 * rows * others + 2 * others * width + VMEM_SPARE),
        cost_estimate=cost_of(rows, width, others),
    )(*blocks)


def products(moving, plane):
    rows, width = moving.shape
    others = plane.shape[0]
    vmem = pl.BlockSpec(memory_space=pltpu.VMEM)
    return pl.pallas_call(
        times_plane,
        out_shape=jax.ShapeDtypeStruct((rows, others), jnp.float32),
        in_specs=[vmem, vmem],
        out_specs=vmem,
        compiler_params=pltpu.CompilerParams(
            vmem_limit_bytes=4 * rows * others + 2 * (rows + others) * width + VMEM_SPARE
        ),
        cost_estimate=cost_of(rows, width, others),
    )(moving, plane)


def maxima_kernel(partners, count, others, two_sided, device, told, moving, plane, *refs):
    tiles = 1 + len(two_sided)
    distant, refs = refs[:others], refs[others:]
    given = dict(zip([0, *range(2, tiles)], refs))
    row_outs = refs[len(given) : len(given) + count]
    column_outs = list(refs[len(given) + count : -2])
    fresh, column_best = refs[-2:]
    rows = moving.shape[0]
    strip = min(STRIP, rows)
    per_block = rows // LANES
    chunk = fresh.shape[2]
    per_chunk = chunk // LANES
    chunks = plane.shape[0] // chunk
    shards = device.shape[0]
    words = -(-shards // WORD)
    source = device[...]
    pairs = [told[:, 2 * rows :]] + [d[0:count, 2 * LANES :] for d in distant]
    table = pair_words(jnp.concatenate(pairs, axis=0), source, partners, words)

    def facts_of(r):
        if r == 0:
            return told[0:1, 0:rows], told[0:1, rows : 2 * rows]
        parts = [distant[r - 1][p : p + 1, 0 : 2 * LANES] for p in range(rows // LANES)]
        return [jnp.concatenate([p[:, at : at + LANES] for p in parts], axis=1) for at in (0, LANES)]

    def bits_of(clusters):
        named = clusters.astype(jnp.int32) == source
        return [jnp.sum(jnp.where(named, t, 0.0), axis=0, keepdims=True).astype(jnp.int32) for t in table]

    def ones_of(at):
        named = told[at : at + 1, rows : 2 * rows].astype(jnp.int32)
        return [jnp.where(named // WORD == w, jnp.int32(1) << (named % WORD), 0) for w in range(words)]

    def along_sublanes(value):
        return jnp.transpose(jnp.broadcast_to(value, (LANES, rows)))

    lane_scale = [told[j : j + 1, 0:rows] for j in range(count)]
    lane_ones = [ones_of(j) for j in range(count)]
    facts = [facts_of(r) for r in range(tiles)]
    scale_down = [along_sublanes(scales) for scales, _ in facts]
    bits_down = [[along_sublanes(b) for b in bits_of(clusters)] for _, clusters in facts]

    def lanes_of(per, g):
        first = g % per_block * LANES
        return per[g // per_block][:, first : first + LANES]

    row_part = {}

    def passed(r, c):
        wants_row = r > 0
        wants_column = r == 0 or two_sided[r - 1]
        for first in range(0, rows, strip):
            here = slice(first, first + strip)
            best = None
            for at in range(per_chunk):
                g = c * per_chunk + at
                if r in given:
                    value = given[r][here, g * LANES : (g + 1) * LANES]
                else:
                    value = fresh[c % 2, here, at * LANES : (at + 1) * LANES]
                met = bits_down[r][0][here] & lanes_of([o[0] for o in lane_ones], g)
                for w in range(1, words):
                    met = met | (bits_down[r][w][here] & lanes_of([o[w] for o in lane_ones], g))
                keep = met != 0
                if r == 0 and g < per_block and g * LANES < first + strip and first < (g + 1) * LANES:
                    down = lax.broadcasted_iota(jnp.int32, value.shape, 0) + first
                    across = lax.broadcasted_iota(jnp.int32, value.shape, 1) + g * LANES
                    keep = keep & (down != across)
                if wants_row:
                    value = jnp.where(keep, value * scale_down[r][here], LOWEST)
                    part = jnp.max(value.reshape(strip // SUBLANES, SUBLANES, LANES), axis=0)
                    row_part[g] = jnp.maximum(row_part[g], part) if g in row_part else part
                    if wants_column:
                        value = value * lanes_of(lane_scale, g)
                else:
                    value = jnp.where(keep, value * lanes_of(lane_scale, g), LOWEST)
                if wants_column:
                    best = value if best is None else jnp.maximum(best, value)
            if wants_column:
                column_best[r, here, :] = best if c == 0 else jnp.maximum(column_best[r, here, :], best)

    for c in range(chunks + 1):
        if c < chunks:
            fresh[c % 2] = lax.dot_general(
                moving[...],
                plane[c * chunk : (c + 1) * chunk, :],
                (((1,), (1,)), ((), ())),
                preferred_element_type=jnp.float32,
            )
            for r in given:
                passed(r, c)
        if c > 0:
            passed(1, c - 1)

    def column_of(r):
        return jnp.max(jnp.transpose(column_best[r]), axis=0, keepdims=True)

    for r in range(1, tiles):
        if two_sided[r - 1]:
            column_outs.pop(0)[...] = column_of(r)
    own_best = column_of(0) * lane_scale[0]
    for j in range(count):
        for at in range(per_block):
            here = slice(at * LANES, (at + 1) * LANES)
            found = jnp.max(row_part[j * per_block + at], axis=0, keepdims=True) * lane_scale[j][:, here]
            if j == 0:
                found = jnp.maximum(found, own_best[:, here])
            row_outs[j][:, here] = found


def maxima(device, told, distant, partners, moving, plane, given, two_sided):
    rows, width = moving.shape
    count = plane.shape[0] // rows
    chunk = min(256, rows)
    vmem = pl.BlockSpec(memory_space=pltpu.VMEM)
    outs = count + sum(two_sided)
    return pl.pallas_call(
        functools.partial(maxima_kernel, partners, count, len(distant), tuple(two_sided)),
        out_shape=[jax.ShapeDtypeStruct((1, rows), jnp.float32)] * outs,
        in_specs=[vmem] * (4 + len(distant) + len(given)),
        out_specs=[vmem] * outs,
        scratch_shapes=[
            pltpu.VMEM((2, rows, chunk), jnp.float32),
            pltpu.VMEM((1 + len(two_sided), rows, LANES), jnp.float32),
        ],
        compiler_params=pltpu.CompilerParams(
            vmem_limit_bytes=4 * rows * plane.shape[0] * len(given)
            + 2 * width * (plane.shape[0] + rows)
            + 2 * VMEM_SPARE
        ),
        cost_estimate=cost_of(rows, width, plane.shape[0]),
    )(device, told, moving, plane, *distant, *given)


def pair_words(listed, source, partners, words):
    shards = listed.shape[0]
    lane = lax.broadcasted_iota(jnp.int32, listed.shape, 1)
    target = source + lane + 1
    used = (lane < partners) & (target < shards) & (listed == 1.0)

    def weight(which, w):
        return jnp.where(which // WORD == w, jnp.int32(1) << (which % WORD), 0).astype(jnp.float32)

    table = []
    for w in range(words):
        met = jnp.where(used, weight(target, w), 0.0) + jnp.where(lane == 0, weight(source, w), 0.0)
        met = jnp.sum(met, axis=1, keepdims=True)
        behind = jnp.where(used, weight(source, w), 0.0)
        for i in range(shards):
            hit = jnp.where(target == source[i : i + 1, :], behind, 0.0)
            here = jnp.sum(jnp.sum(hit, axis=0, keepdims=True), axis=1, keepdims=True)
            met = met + jnp.where(lax.broadcasted_iota(jnp.int32, met.shape, 0) == i, here, 0.0)
        table.append(met)
    return table


def kept_kernel(value, after, out):
    out[...] = value[...]


def kept(value, after):
    vmem = pl.BlockSpec(memory_space=pltpu.VMEM)
    return pl.pallas_call(
        kept_kernel,
        out_shape=jax.ShapeDtypeStruct(value.shape, value.dtype),
        in_specs=[vmem, pl.BlockSpec(memory_space=pl.ANY)],
        out_specs=vmem,
        compiler_params=pltpu.CompilerParams(vmem_limit_bytes=2**20),
    )(value, after)


def joined_kernel(plane, *refs):
    pieces, told, packed = refs[:-3], refs[-2], refs[-1]
    at = 0
    for piece in pieces:
        told[at : at + piece.shape[0], :] = piece[...]
        at += piece.shape[0]
    rows = packed.shape[1] - 2 * LANES
    facts = (pieces[0].shape[1] - rows) // 2
    packed[...] = jnp.zeros(packed.shape, packed.dtype)
    for part in range(facts // LANES):
        here = slice(part * LANES, (part + 1) * LANES)
        packed[part : part + 1, 0:LANES] = pieces[0][0:1, here]
        packed[part : part + 1, LANES : 2 * LANES] = pieces[0][0:1, facts + part * LANES : facts + (part + 1) * LANES]
    packed[0:plane, 2 * LANES :] = told[0:plane, 2 * facts :]


def joined(pieces, facts, after):
    vmem = pl.BlockSpec(memory_space=pltpu.VMEM)
    length = pieces[0].shape[1]
    plane = sum(p.shape[0] for p in pieces)
    return pl.pallas_call(
        functools.partial(joined_kernel, plane),
        out_shape=[
            jax.ShapeDtypeStruct((plane, length), jnp.float32),
            jax.ShapeDtypeStruct((max(plane, facts // LANES), length - 2 * facts + 2 * LANES), jnp.float32),
        ],
        in_specs=[vmem] * len(pieces) + [pl.BlockSpec(memory_space=pl.ANY)],
        out_specs=[vmem, vmem],
        compiler_params=pltpu.CompilerParams(vmem_limit_bytes=2**20),
    )(*pieces, after)


def device_table(shards, plane, planes, order, place_of, here):
    rel = jnp.arange(shards, dtype=jnp.int32)
    place = jnp.sum(jnp.where(jnp.arange(planes) == here // plane, jnp.asarray(place_of, jnp.int32), 0))
    place = (place - rel // plane) % planes
    z = jnp.sum(jnp.where(place[:, None] == jnp.arange(planes)[None, :], jnp.asarray(order, jnp.int32)[None, :], 0), axis=1)
    return (z * plane + (here % plane ^ rel % plane)).reshape(shards, 1)


def per_device(embeddings, scales, cluster, pair_listed):
    rows, width = embeddings.shape
    shards = lax.axis_size("shard")
    here = lax.axis_index("shard")
    plane = 1
    while plane * plane * 4 <= shards:
        plane *= 2
    planes = shards // plane
    half = planes // 2
    owned, partners = pair_listed.shape

    order = [place // 2 + (place % 2) * half for place in range(planes)]
    place_of = [order.index(z) for z in range(planes)]

    def permuted(value, target):
        return lax.ppermute(value, "shard", [(s, target(s)) for s in range(shards)])

    def across(bit):
        return lambda s: s ^ bit

    def along(distance):
        def target(s):
            z = order[(place_of[s // plane] + distance) % planes]
            return z * plane + s % plane

        return target

    arrived = {}
    for distance in range(1, half + 1):
        arrived[distance] = permuted(embeddings, along(distance))
    parts = 2
    size = rows // parts
    held = {(0, p): embeddings[p * size : (p + 1) * size] for p in range(parts)}
    whole_block = {0: embeddings}
    bit = plane // 2
    while bit:
        for j, p in sorted(held):
            if bit == 1 and j == 0:
                continue
            held[j | bit, p] = permuted(held[j, p], across(bit))
        bit //= 2
    whole_block[1] = permuted(embeddings, across(1))
    blocks = []
    for j in range(plane):
        blocks += [whole_block[j]] if j in whole_block else [held[j, p] for p in range(parts)]

    pairs = jnp.pad(pair_listed.reshape(-1).astype(jnp.float32), (0, -(owned * partners) % LANES))
    told = jnp.concatenate([scales.astype(jnp.float32), cluster[:, 0].astype(jnp.float32), pairs])[None, :]
    told = kept(told, held[plane // 2, 0])
    pieces, bit = [told], 1
    while bit < plane:
        mine = pieces[0] if len(pieces) == 1 else jnp.concatenate(pieces, axis=0)
        pieces.append(permuted(mine, across(bit)))
        bit *= 2
    raw, whole = gathered_plane(blocks)
    told, packed = joined(pieces, rows, raw)
    distant = [permuted(packed, along(t)) for t in range(1, planes)]
    device = device_table(shards, plane, planes, order, place_of, here)
    distances = range(1, half + 1)
    two_sided = [2 * distance != planes for distance in distances]
    given = [raw] + [products(arrived[distance], whole) for distance in distances[1:]]
    found = maxima(device, told, distant, partners, arrived[1], whole, given, two_sided)
    gathered, columns = found[:plane], list(found[plane:])

    result = gathered[0]
    returned = []
    for distance in distances:
        if two_sided[distance - 1]:
            returned.append(permuted(columns.pop(0), along(-distance)))
    returned += [permuted(gathered[j], across(j)) for j in range(plane - 1, 0, -1)]
    return functools.reduce(jnp.maximum, returned, result).reshape(rows)


def solution(mesh):
    placed = (
        P(("groups", "shard"), None),
        P(("groups", "shard")),
        P(("groups", "shard"), None),
        P(("groups", "shard"), None),
    )
    return jax.shard_map(
        per_device, mesh=mesh, in_specs=placed, out_specs=P(("groups", "shard")), check_vma=False
    )
```

```python
import functools

import jax
import jax.numpy as jnp
from jax import lax
from jax.experimental import pallas as pl
from jax.experimental.pallas import tpu as pltpu
from jax.sharding import PartitionSpec as P

LOWEST = float("-inf")
WORD = 16
LANES = 128
SUBLANES = 8
STRIP = 64
VMEM_SPARE = 4 * 2**20


def gather_kernel(count, *refs):
    blocks = refs[:count]
    out, turned, plane, arrived = refs[count:]
    rows = blocks[0].shape[0]
    copies, at = [], 0
    for j, block in enumerate(blocks):
        copies.append(pltpu.make_async_copy(block, plane.at[at : at + block.shape[0], :], arrived.at[j]))
        at += block.shape[0]
    for copy in copies:
        copy.start()
    for copy in copies:
        copy.wait()
    first_part = out.shape[1]
    times_plane(plane.at[:rows, :], plane.at[:first_part, :], out)
    chunk = min(256, rows)
    for first in range(first_part, plane.shape[0], chunk):
        turned[first - first_part : first - first_part + chunk, :] = lax.dot_general(
            plane[first : first + chunk, :],
            plane[:rows, :],
            (((1,), (1,)), ((), ())),
            preferred_element_type=jnp.float32,
        )


def product_kernel(moving, plane, after, out):
    times_plane(moving, plane, out)


def times_plane(moving, plane, out):
    chunk = min(256, moving.shape[0])
    for first in range(0, plane.shape[0], chunk):
        out[:, first : first + chunk] = lax.dot_general(
            moving[...],
            plane[first : first + chunk, :],
            (((1,), (1,)), ((), ())),
            preferred_element_type=jnp.float32,
        )


def cost_of(rows, width, others):
    return pl.CostEstimate(
        flops=2 * rows * others * width, bytes_accessed=2 * (rows + others) * width, transcendentals=0
    )


def gathered_plane(blocks):
    rows, width = blocks[0].shape
    others = sum(block.shape[0] for block in blocks)
    vmem = pl.BlockSpec(memory_space=pltpu.VMEM)
    return pl.pallas_call(
        functools.partial(gather_kernel, len(blocks)),
        out_shape=[
            jax.ShapeDtypeStruct((rows, others // 2), jnp.float32),
            jax.ShapeDtypeStruct((others - others // 2, rows), jnp.float32),
            jax.ShapeDtypeStruct((others, width), blocks[0].dtype),
        ],
        in_specs=[pl.BlockSpec(memory_space=pl.ANY)] * len(blocks),
        out_specs=[vmem] * 3,
        scratch_shapes=[pltpu.SemaphoreType.DMA((len(blocks),))],
        compiler_params=pltpu.CompilerParams(vmem_limit_bytes=4 * rows * others + 2 * others * width + VMEM_SPARE),
        cost_estimate=cost_of(rows, width, others),
    )(*blocks)


def products(moving, plane, after):
    rows, width = moving.shape
    others = plane.shape[0]
    vmem = pl.BlockSpec(memory_space=pltpu.VMEM)
    return pl.pallas_call(
        product_kernel,
        out_shape=jax.ShapeDtypeStruct((rows, others), jnp.float32),
        in_specs=[vmem, vmem, pl.BlockSpec(memory_space=pl.ANY)],
        out_specs=vmem,
        compiler_params=pltpu.CompilerParams(
            vmem_limit_bytes=4 * rows * others + 2 * (rows + others) * width + VMEM_SPARE
        ),
        cost_estimate=cost_of(rows, width, others),
    )(moving, plane, after)


def along_sublanes(value):
    return jnp.transpose(jnp.broadcast_to(value, (LANES, value.shape[1])))


def classes_kernel(partners, told, raw, out, scale_down, cluster_down):
    count, rows = told.shape[0], raw.shape[1]
    strip = min(STRIP, rows)
    blocks = raw.shape[0] // rows
    for i in range(blocks):
        j = count - blocks + i
        here = slice(i * rows, (i + 1) * rows)
        scale_down[here, :] = along_sublanes(told[j : j + 1, 0:rows])
        cluster_down[here, :] = along_sublanes(told[j : j + 1, rows : 2 * rows])
    offsets = range(-partners, partners + 1)
    for first in range(0, rows, LANES):
        mine = told[0:1, rows + first : rows + first + LANES]

        def step(i, best):
            here = pl.ds(pl.multiple_of(i * strip, strip), strip)
            value = raw[here, first : first + LANES] * scale_down[here, :]
            ahead = cluster_down[here, :] - mine
            found = []
            for before, offset in zip(best, offsets):
                one = jnp.where(ahead == float(offset), value, LOWEST)
                one = jnp.max(one.reshape(strip // SUBLANES, SUBLANES, LANES), axis=0)
                found.append(jnp.maximum(before, one))
            return tuple(found)

        start = tuple(jnp.full((SUBLANES, LANES), LOWEST, jnp.float32) for _ in offsets)
        best = lax.fori_loop(0, raw.shape[0] // strip, step, start)
        for k, one in enumerate(best):
            out[k : k + 1, first : first + LANES] = jnp.max(one, axis=0, keepdims=True)


def classes(told, raw, partners):
    others, rows = raw.shape
    vmem = pl.BlockSpec(memory_space=pltpu.VMEM)
    return pl.pallas_call(
        functools.partial(classes_kernel, partners),
        out_shape=jax.ShapeDtypeStruct((2 * partners + 1, rows), jnp.float32),
        in_specs=[vmem, vmem],
        out_specs=vmem,
        scratch_shapes=[pltpu.VMEM((others, LANES), jnp.float32)] * 2,
        compiler_params=pltpu.CompilerParams(vmem_limit_bytes=4 * others * (rows + 2 * LANES) + VMEM_SPARE),
    )(told, raw)


def maxima_kernel(partners, count, others, two_sided, device, told, own_classes, moving, plane, *refs):
    tiles = 1 + len(two_sided)
    distant, refs = refs[:others], refs[others:]
    given = dict(zip([0, *range(2, tiles)], refs))
    row_outs = refs[len(given) : len(given) + count]
    column_outs = list(refs[len(given) + count : -2])
    fresh, column_best = refs[-2:]
    rows = moving.shape[0]
    strip = min(STRIP, rows)
    per_block = rows // LANES
    chunk = fresh.shape[2]
    per_chunk = chunk // LANES
    chunks = plane.shape[0] // chunk
    shards = device.shape[0]
    words = -(-shards // WORD)
    source = device[...]
    pairs = [told[:, 2 * rows :]] + [d[0:count, 2 * LANES :] for d in distant]
    table = pair_words(jnp.concatenate(pairs, axis=0), source, partners, words)

    def facts_of(r):
        if r == 0:
            return told[0:1, 0:rows], told[0:1, rows : 2 * rows]
        parts = [distant[r - 1][p : p + 1, 0 : 2 * LANES] for p in range(rows // LANES)]
        return [jnp.concatenate([p[:, at : at + LANES] for p in parts], axis=1) for at in (0, LANES)]

    def bits_of(clusters):
        named = clusters.astype(jnp.int32) == source
        return [jnp.sum(jnp.where(named, t, 0.0), axis=0, keepdims=True).astype(jnp.int32) for t in table]

    def ones_of(at):
        named = told[at : at + 1, rows : 2 * rows].astype(jnp.int32)
        return [jnp.where(named // WORD == w, jnp.int32(1) << (named % WORD), 0) for w in range(words)]

    lane_scale = [told[j : j + 1, 0:rows] for j in range(count)]
    lane_ones = [ones_of(j) for j in range(count)]
    facts = [facts_of(r) for r in range(tiles)]
    scale_down = [along_sublanes(scales) for scales, _ in facts]
    bits_down = [[along_sublanes(b) for b in bits_of(clusters)] for _, clusters in facts]

    def lanes_of(per, g):
        first = g % per_block * LANES
        return per[g // per_block][:, first : first + LANES]

    row_part = {}

    def passed(r, c):
        wants_row = r > 0
        wants_column = r == 0 or two_sided[r - 1]
        for first in range(0, rows, strip):
            here = slice(first, first + strip)
            best = None
            for at in range(per_chunk):
                g = c * per_chunk + at
                if r in given:
                    value = given[r][here, g * LANES : (g + 1) * LANES]
                else:
                    value = fresh[c % 2, here, at * LANES : (at + 1) * LANES]
                met = bits_down[r][0][here] & lanes_of([o[0] for o in lane_ones], g)
                for w in range(1, words):
                    met = met | (bits_down[r][w][here] & lanes_of([o[w] for o in lane_ones], g))
                keep = met != 0
                if r == 0 and g < per_block and g * LANES < first + strip and first < (g + 1) * LANES:
                    down = lax.broadcasted_iota(jnp.int32, value.shape, 0) + first
                    across = lax.broadcasted_iota(jnp.int32, value.shape, 1) + g * LANES
                    keep = keep & (down != across)
                if wants_row:
                    value = jnp.where(keep, value * scale_down[r][here], LOWEST)
                    part = jnp.max(value.reshape(strip // SUBLANES, SUBLANES, LANES), axis=0)
                    row_part[g] = jnp.maximum(row_part[g], part) if g in row_part else part
                    if wants_column:
                        value = value * lanes_of(lane_scale, g)
                else:
                    value = jnp.where(keep, value * lanes_of(lane_scale, g), LOWEST)
                if wants_column:
                    best = value if best is None else jnp.maximum(best, value)
            if wants_column:
                column_best[r, here, :] = best if c == 0 else jnp.maximum(column_best[r, here, :], best)

    for c in range(chunks + 1):
        if c < chunks:
            fresh[c % 2] = lax.dot_general(
                moving[...],
                plane[c * chunk : (c + 1) * chunk, :],
                (((1,), (1,)), ((), ())),
                preferred_element_type=jnp.float32,
            )
            for r in given:
                if c * chunk < given[r].shape[1]:
                    passed(r, c)
        if c > 0:
            passed(1, c - 1)

    def column_of(r):
        return jnp.max(jnp.transpose(column_best[r]), axis=0, keepdims=True)

    for r in range(1, tiles):
        if two_sided[r - 1]:
            column_outs.pop(0)[...] = column_of(r)
    own_best = column_of(0)
    own_bits = bits_of(facts[0][1])
    named = facts[0][1].astype(jnp.int32)
    for k in range(2 * partners + 1):
        met = jnp.int32(0)
        other = named + (k - partners)
        for w in range(words):
            bit = jnp.where((other >= 0) & (other // WORD == w), jnp.int32(1) << (other % WORD), 0)
            met = met | (own_bits[w] & bit)
        own_best = jnp.maximum(own_best, jnp.where(met != 0, own_classes[k : k + 1, :], LOWEST))
    own_best = own_best * lane_scale[0]
    for j in range(count):
        for at in range(per_block):
            here = slice(at * LANES, (at + 1) * LANES)
            found = jnp.max(row_part[j * per_block + at], axis=0, keepdims=True) * lane_scale[j][:, here]
            if j == 0:
                found = jnp.maximum(found, own_best[:, here])
            row_outs[j][:, here] = found


def maxima(device, told, own_classes, distant, partners, moving, plane, given, two_sided):
    rows, width = moving.shape
    count = plane.shape[0] // rows
    chunk = min(256, rows)
    vmem = pl.BlockSpec(memory_space=pltpu.VMEM)
    outs = count + sum(two_sided)
    return pl.pallas_call(
        functools.partial(maxima_kernel, partners, count, len(distant), tuple(two_sided)),
        out_shape=[jax.ShapeDtypeStruct((1, rows), jnp.float32)] * outs,
        in_specs=[vmem] * (5 + len(distant) + len(given)),
        out_specs=[vmem] * outs,
        scratch_shapes=[
            pltpu.VMEM((2, rows, chunk), jnp.float32),
            pltpu.VMEM((1 + len(two_sided), rows, LANES), jnp.float32),
        ],
        compiler_params=pltpu.CompilerParams(
            vmem_limit_bytes=4 * rows * plane.shape[0] * len(given)
            + 2 * width * (plane.shape[0] + rows)
            + 2 * VMEM_SPARE
        ),
        cost_estimate=cost_of(rows, width, plane.shape[0]),
    )(device, told, own_classes, moving, plane, *distant, *given)


def pair_words(listed, source, partners, words):
    shards = listed.shape[0]
    lane = lax.broadcasted_iota(jnp.int32, listed.shape, 1)
    target = source + lane + 1
    used = (lane < partners) & (target < shards) & (listed == 1.0)

    def weight(which, w):
        return jnp.where(which // WORD == w, jnp.int32(1) << (which % WORD), 0).astype(jnp.float32)

    table = []
    for w in range(words):
        met = jnp.where(used, weight(target, w), 0.0) + jnp.where(lane == 0, weight(source, w), 0.0)
        met = jnp.sum(met, axis=1, keepdims=True)
        behind = jnp.where(used, weight(source, w), 0.0)
        for i in range(shards):
            hit = jnp.where(target == source[i : i + 1, :], behind, 0.0)
            here = jnp.sum(jnp.sum(hit, axis=0, keepdims=True), axis=1, keepdims=True)
            met = met + jnp.where(lax.broadcasted_iota(jnp.int32, met.shape, 0) == i, here, 0.0)
        table.append(met)
    return table


def kept_kernel(value, after, out):
    out[...] = value[...]


def kept(value, after):
    vmem = pl.BlockSpec(memory_space=pltpu.VMEM)
    return pl.pallas_call(
        kept_kernel,
        out_shape=jax.ShapeDtypeStruct(value.shape, value.dtype),
        in_specs=[vmem, pl.BlockSpec(memory_space=pl.ANY)],
        out_specs=vmem,
        compiler_params=pltpu.CompilerParams(vmem_limit_bytes=2**20),
    )(value, after)


def joined_kernel(plane, *refs):
    pieces, told, packed = refs[:-3], refs[-2], refs[-1]
    at = 0
    for piece in pieces:
        told[at : at + piece.shape[0], :] = piece[...]
        at += piece.shape[0]
    rows = packed.shape[1] - 2 * LANES
    facts = (pieces[0].shape[1] - rows) // 2
    packed[...] = jnp.zeros(packed.shape, packed.dtype)
    for part in range(facts // LANES):
        here = slice(part * LANES, (part + 1) * LANES)
        packed[part : part + 1, 0:LANES] = pieces[0][0:1, here]
        packed[part : part + 1, LANES : 2 * LANES] = pieces[0][0:1, facts + part * LANES : facts + (part + 1) * LANES]
    packed[0:plane, 2 * LANES :] = told[0:plane, 2 * facts :]


def joined(pieces, facts, after):
    vmem = pl.BlockSpec(memory_space=pltpu.VMEM)
    length = pieces[0].shape[1]
    plane = sum(p.shape[0] for p in pieces)
    return pl.pallas_call(
        functools.partial(joined_kernel, plane),
        out_shape=[
            jax.ShapeDtypeStruct((plane, length), jnp.float32),
            jax.ShapeDtypeStruct((max(plane, facts // LANES), length - 2 * facts + 2 * LANES), jnp.float32),
        ],
        in_specs=[vmem] * len(pieces) + [pl.BlockSpec(memory_space=pl.ANY)],
        out_specs=[vmem, vmem],
        compiler_params=pltpu.CompilerParams(vmem_limit_bytes=2**20),
    )(*pieces, after)


def device_table(shards, plane, planes, order, place_of, here):
    rel = jnp.arange(shards, dtype=jnp.int32)
    place = jnp.sum(jnp.where(jnp.arange(planes) == here // plane, jnp.asarray(place_of, jnp.int32), 0))
    place = (place - rel // plane) % planes
    z = jnp.sum(jnp.where(place[:, None] == jnp.arange(planes)[None, :], jnp.asarray(order, jnp.int32)[None, :], 0), axis=1)
    return (z * plane + (here % plane ^ rel % plane)).reshape(shards, 1)


def per_device(embeddings, scales, cluster, pair_listed):
    rows, width = embeddings.shape
    shards = lax.axis_size("shard")
    here = lax.axis_index("shard")
    plane = 1
    while plane * plane * 4 <= shards:
        plane *= 2
    planes = shards // plane
    half = planes // 2
    owned, partners = pair_listed.shape

    order = [place // 2 + (place % 2) * half for place in range(planes)]
    place_of = [order.index(z) for z in range(planes)]

    def permuted(value, target):
        return lax.ppermute(value, "shard", [(s, target(s)) for s in range(shards)])

    def across(bit):
        return lambda s: s ^ bit

    def along(distance):
        def target(s):
            z = order[(place_of[s // plane] + distance) % planes]
            return z * plane + s % plane

        return target

    arrived = {}
    for distance in range(1, half + 1):
        arrived[distance] = permuted(embeddings, along(distance))
    parts = 2
    size = rows // parts
    held = {(0, p): embeddings[p * size : (p + 1) * size] for p in range(parts)}
    whole_block = {0: embeddings}
    bit = plane // 2
    while bit:
        for j, p in sorted(held):
            if bit == 1 and j == 0:
                continue
            held[j | bit, p] = permuted(held[j, p], across(bit))
        bit //= 2
    whole_block[1] = permuted(embeddings, across(1))
    blocks = []
    for j in range(plane):
        blocks += [whole_block[j]] if j in whole_block else [held[j, p] for p in range(parts)]

    pairs = jnp.pad(pair_listed.reshape(-1).astype(jnp.float32), (0, -(owned * partners) % LANES))
    told = jnp.concatenate([scales.astype(jnp.float32), cluster[:, 0].astype(jnp.float32), pairs])[None, :]
    told = kept(told, held[plane // 2, 0])
    pieces, bit = [told], 1
    while bit < plane:
        mine = pieces[0] if len(pieces) == 1 else jnp.concatenate(pieces, axis=0)
        pieces.append(permuted(mine, across(bit)))
        bit *= 2
    raw, turned, whole = gathered_plane(blocks)
    told, packed = joined(pieces, rows, raw)
    distant = [permuted(packed, along(t)) for t in range(1, planes)]
    device = device_table(shards, plane, planes, order, place_of, here)
    distances = range(1, half + 1)
    two_sided = [2 * distance != planes for distance in distances]
    own_classes = classes(told, turned, partners)
    given = [raw] + [products(arrived[distance], whole, own_classes) for distance in distances[1:]]
    found = maxima(device, told, own_classes, distant, partners, arrived[1], whole, given, two_sided)
    gathered, columns = found[:plane], list(found[plane:])

    result = gathered[0]
    returned = []
    for distance in distances:
        if two_sided[distance - 1]:
            returned.append(permuted(columns.pop(0), along(-distance)))
    returned += [permuted(gathered[j], across(j)) for j in range(plane - 1, 0, -1)]
    return functools.reduce(jnp.maximum, returned, result).reshape(rows)


def solution(mesh):
    placed = (
        P(("groups", "shard"), None),
        P(("groups", "shard")),
        P(("groups", "shard"), None),
        P(("groups", "shard"), None),
    )
    return jax.shard_map(
        per_device, mesh=mesh, in_specs=placed, out_specs=P(("groups", "shard")), check_vma=False
    )
```

```python
import functools

import jax
import jax.numpy as jnp
from jax import lax
from jax.experimental import pallas as pl
from jax.experimental.pallas import tpu as pltpu
from jax.sharding import PartitionSpec as P

LOWEST = float("-inf")
WORD = 16
LANES = 128
SUBLANES = 8
STRIP = 64
VMEM_SPARE = 4 * 2**20


def gather_kernel(count, *refs):
    blocks = refs[:count]
    out, turned, plane, arrived = refs[count:]
    rows = blocks[0].shape[0]
    copies, at = [], 0
    for j, block in enumerate(blocks):
        copies.append(pltpu.make_async_copy(block, plane.at[at : at + block.shape[0], :], arrived.at[j]))
        at += block.shape[0]
    for copy in copies:
        copy.start()
    first_part = out.shape[1]
    starts = [sum(block.shape[0] for block in blocks[:j]) for j in range(count)]
    for copy, start in zip(copies, starts):
        if start < first_part:
            copy.wait()
    times_plane(plane.at[:rows, :], plane.at[:first_part, :], out)
    for copy, start in zip(copies, starts):
        if start >= first_part:
            copy.wait()
    chunk = min(256, rows)
    for first in range(first_part, plane.shape[0], chunk):
        turned[first - first_part : first - first_part + chunk, :] = lax.dot_general(
            plane[first : first + chunk, :],
            plane[:rows, :],
            (((1,), (1,)), ((), ())),
            preferred_element_type=jnp.float32,
        )


def product_kernel(moving, plane, after, out):
    times_plane(moving, plane, out)


def times_plane(moving, plane, out):
    chunk = min(256, moving.shape[0])
    for first in range(0, plane.shape[0], chunk):
        out[:, first : first + chunk] = lax.dot_general(
            moving[...],
            plane[first : first + chunk, :],
            (((1,), (1,)), ((), ())),
            preferred_element_type=jnp.float32,
        )


def cost_of(rows, width, others):
    return pl.CostEstimate(
        flops=2 * rows * others * width, bytes_accessed=2 * (rows + others) * width, transcendentals=0
    )


def gathered_plane(blocks):
    rows, width = blocks[0].shape
    others = sum(block.shape[0] for block in blocks)
    vmem = pl.BlockSpec(memory_space=pltpu.VMEM)
    return pl.pallas_call(
        functools.partial(gather_kernel, len(blocks)),
        out_shape=[
            jax.ShapeDtypeStruct((rows, others // 2), jnp.float32),
            jax.ShapeDtypeStruct((others - others // 2, rows), jnp.float32),
            jax.ShapeDtypeStruct((others, width), blocks[0].dtype),
        ],
        in_specs=[pl.BlockSpec(memory_space=pl.ANY)] * len(blocks),
        out_specs=[vmem] * 3,
        scratch_shapes=[pltpu.SemaphoreType.DMA((len(blocks),))],
        compiler_params=pltpu.CompilerParams(vmem_limit_bytes=4 * rows * others + 2 * others * width + VMEM_SPARE),
        cost_estimate=cost_of(rows, width, others),
    )(*blocks)


def products(moving, plane, after):
    rows, width = moving.shape
    others = plane.shape[0]
    vmem = pl.BlockSpec(memory_space=pltpu.VMEM)
    return pl.pallas_call(
        product_kernel,
        out_shape=jax.ShapeDtypeStruct((rows, others), jnp.float32),
        in_specs=[vmem, vmem, pl.BlockSpec(memory_space=pl.ANY)],
        out_specs=vmem,
        compiler_params=pltpu.CompilerParams(
            vmem_limit_bytes=4 * rows * others + 2 * (rows + others) * width + VMEM_SPARE
        ),
        cost_estimate=cost_of(rows, width, others),
    )(moving, plane, after)


def along_sublanes(value):
    return jnp.transpose(jnp.broadcast_to(value, (LANES, value.shape[1])))


def classes_kernel(partners, told, raw, out, scale_down, cluster_down):
    count, rows = told.shape[0], raw.shape[1]
    strip = min(STRIP, rows)
    blocks = raw.shape[0] // rows
    for i in range(blocks):
        j = count - blocks + i
        here = slice(i * rows, (i + 1) * rows)
        scale_down[here, :] = along_sublanes(told[j : j + 1, 0:rows])
        cluster_down[here, :] = along_sublanes(told[j : j + 1, rows : 2 * rows])
    offsets = range(-partners, partners + 1)
    for first in range(0, rows, LANES):
        mine = told[0:1, rows + first : rows + first + LANES]

        def step(i, best):
            here = pl.ds(pl.multiple_of(i * strip, strip), strip)
            value = raw[here, first : first + LANES] * scale_down[here, :]
            ahead = cluster_down[here, :] - mine
            found = []
            for before, offset in zip(best, offsets):
                one = jnp.where(ahead == float(offset), value, LOWEST)
                one = jnp.max(one.reshape(strip // SUBLANES, SUBLANES, LANES), axis=0)
                found.append(jnp.maximum(before, one))
            return tuple(found)

        start = tuple(jnp.full((SUBLANES, LANES), LOWEST, jnp.float32) for _ in offsets)
        best = lax.fori_loop(0, raw.shape[0] // strip, step, start)
        for k, one in enumerate(best):
            out[k : k + 1, first : first + LANES] = jnp.max(one, axis=0, keepdims=True)


def classes(told, raw, partners):
    others, rows = raw.shape
    vmem = pl.BlockSpec(memory_space=pltpu.VMEM)
    return pl.pallas_call(
        functools.partial(classes_kernel, partners),
        out_shape=jax.ShapeDtypeStruct((2 * partners + 1, rows), jnp.float32),
        in_specs=[vmem, vmem],
        out_specs=vmem,
        scratch_shapes=[pltpu.VMEM((others, LANES), jnp.float32)] * 2,
        compiler_params=pltpu.CompilerParams(vmem_limit_bytes=4 * others * (rows + 2 * LANES) + VMEM_SPARE),
    )(told, raw)


def maxima_kernel(partners, count, others, two_sided, device, told, own_classes, moving, plane, *refs):
    tiles = 1 + len(two_sided)
    distant, refs = refs[:others], refs[others:]
    given = dict(zip([0, *range(2, tiles)], refs))
    row_outs = refs[len(given) : len(given) + count]
    column_outs = list(refs[len(given) + count : -2])
    fresh, column_best = refs[-2:]
    rows = moving.shape[0]
    strip = min(STRIP, rows)
    per_block = rows // LANES
    chunk = fresh.shape[2]
    per_chunk = chunk // LANES
    chunks = plane.shape[0] // chunk
    shards = device.shape[0]
    words = -(-shards // WORD)
    source = device[...]
    pairs = [told[:, 2 * rows :]] + [d[0:count, 2 * LANES :] for d in distant]
    table = pair_words(jnp.concatenate(pairs, axis=0), source, partners, words)

    def facts_of(r):
        if r == 0:
            return told[0:1, 0:rows], told[0:1, rows : 2 * rows]
        parts = [distant[r - 1][p : p + 1, 0 : 2 * LANES] for p in range(rows // LANES)]
        return [jnp.concatenate([p[:, at : at + LANES] for p in parts], axis=1) for at in (0, LANES)]

    def bits_of(clusters):
        named = clusters.astype(jnp.int32) == source
        return [jnp.sum(jnp.where(named, t, 0.0), axis=0, keepdims=True).astype(jnp.int32) for t in table]

    def ones_of(at):
        named = told[at : at + 1, rows : 2 * rows].astype(jnp.int32)
        return [jnp.where(named // WORD == w, jnp.int32(1) << (named % WORD), 0) for w in range(words)]

    lane_scale = [told[j : j + 1, 0:rows] for j in range(count)]
    lane_ones = [ones_of(j) for j in range(count)]
    facts = [facts_of(r) for r in range(tiles)]
    scale_down = [along_sublanes(scales) for scales, _ in facts]
    bits_down = [[along_sublanes(b) for b in bits_of(clusters)] for _, clusters in facts]

    def lanes_of(per, g):
        first = g % per_block * LANES
        return per[g // per_block][:, first : first + LANES]

    row_part = {}

    def passed(r, c):
        wants_row = r > 0
        wants_column = r == 0 or two_sided[r - 1]
        for first in range(0, rows, strip):
            here = slice(first, first + strip)
            best = None
            for at in range(per_chunk):
                g = c * per_chunk + at
                if r in given:
                    value = given[r][here, g * LANES : (g + 1) * LANES]
                else:
                    value = fresh[c % 2, here, at * LANES : (at + 1) * LANES]
                met = bits_down[r][0][here] & lanes_of([o[0] for o in lane_ones], g)
                for w in range(1, words):
                    met = met | (bits_down[r][w][here] & lanes_of([o[w] for o in lane_ones], g))
                keep = met != 0
                if r == 0 and g < per_block and g * LANES < first + strip and first < (g + 1) * LANES:
                    down = lax.broadcasted_iota(jnp.int32, value.shape, 0) + first
                    across = lax.broadcasted_iota(jnp.int32, value.shape, 1) + g * LANES
                    keep = keep & (down != across)
                if wants_row:
                    value = jnp.where(keep, value * scale_down[r][here], LOWEST)
                    part = jnp.max(value.reshape(strip // SUBLANES, SUBLANES, LANES), axis=0)
                    row_part[g] = jnp.maximum(row_part[g], part) if g in row_part else part
                    if wants_column:
                        value = value * lanes_of(lane_scale, g)
                else:
                    value = jnp.where(keep, value * lanes_of(lane_scale, g), LOWEST)
                if wants_column:
                    best = value if best is None else jnp.maximum(best, value)
            if wants_column:
                column_best[r, here, :] = best if c == 0 else jnp.maximum(column_best[r, here, :], best)

    for c in range(chunks + 1):
        if c < chunks:
            fresh[c % 2] = lax.dot_general(
                moving[...],
                plane[c * chunk : (c + 1) * chunk, :],
                (((1,), (1,)), ((), ())),
                preferred_element_type=jnp.float32,
            )
            for r in given:
                if c * chunk < given[r].shape[1]:
                    passed(r, c)
        if c > 0:
            passed(1, c - 1)

    def column_of(r):
        return jnp.max(jnp.transpose(column_best[r]), axis=0, keepdims=True)

    for r in range(1, tiles):
        if two_sided[r - 1]:
            column_outs.pop(0)[...] = column_of(r)
    own_best = column_of(0)
    own_bits = bits_of(facts[0][1])
    named = facts[0][1].astype(jnp.int32)
    for k in range(2 * partners + 1):
        met = jnp.int32(0)
        other = named + (k - partners)
        for w in range(words):
            bit = jnp.where((other >= 0) & (other // WORD == w), jnp.int32(1) << (other % WORD), 0)
            met = met | (own_bits[w] & bit)
        own_best = jnp.maximum(own_best, jnp.where(met != 0, own_classes[k : k + 1, :], LOWEST))
    own_best = own_best * lane_scale[0]
    for j in range(count):
        for at in range(per_block):
            here = slice(at * LANES, (at + 1) * LANES)
            found = jnp.max(row_part[j * per_block + at], axis=0, keepdims=True) * lane_scale[j][:, here]
            if j == 0:
                found = jnp.maximum(found, own_best[:, here])
            row_outs[j][:, here] = found


def maxima(device, told, own_classes, distant, partners, moving, plane, given, two_sided):
    rows, width = moving.shape
    count = plane.shape[0] // rows
    chunk = min(256, rows)
    vmem = pl.BlockSpec(memory_space=pltpu.VMEM)
    outs = count + sum(two_sided)
    return pl.pallas_call(
        functools.partial(maxima_kernel, partners, count, len(distant), tuple(two_sided)),
        out_shape=[jax.ShapeDtypeStruct((1, rows), jnp.float32)] * outs,
        in_specs=[vmem] * (5 + len(distant) + len(given)),
        out_specs=[vmem] * outs,
        scratch_shapes=[
            pltpu.VMEM((2, rows, chunk), jnp.float32),
            pltpu.VMEM((1 + len(two_sided), rows, LANES), jnp.float32),
        ],
        compiler_params=pltpu.CompilerParams(
            vmem_limit_bytes=4 * rows * plane.shape[0] * len(given)
            + 2 * width * (plane.shape[0] + rows)
            + 2 * VMEM_SPARE
        ),
        cost_estimate=cost_of(rows, width, plane.shape[0]),
    )(device, told, own_classes, moving, plane, *distant, *given)


def pair_words(listed, source, partners, words):
    shards = listed.shape[0]
    lane = lax.broadcasted_iota(jnp.int32, listed.shape, 1)
    target = source + lane + 1
    used = (lane < partners) & (target < shards) & (listed == 1.0)

    def weight(which, w):
        return jnp.where(which // WORD == w, jnp.int32(1) << (which % WORD), 0).astype(jnp.float32)

    table = []
    for w in range(words):
        met = jnp.where(used, weight(target, w), 0.0) + jnp.where(lane == 0, weight(source, w), 0.0)
        met = jnp.sum(met, axis=1, keepdims=True)
        behind = jnp.where(used, weight(source, w), 0.0)
        for i in range(shards):
            hit = jnp.where(target == source[i : i + 1, :], behind, 0.0)
            here = jnp.sum(jnp.sum(hit, axis=0, keepdims=True), axis=1, keepdims=True)
            met = met + jnp.where(lax.broadcasted_iota(jnp.int32, met.shape, 0) == i, here, 0.0)
        table.append(met)
    return table


def kept_kernel(value, after, out):
    out[...] = value[...]


def kept(value, after):
    vmem = pl.BlockSpec(memory_space=pltpu.VMEM)
    return pl.pallas_call(
        kept_kernel,
        out_shape=jax.ShapeDtypeStruct(value.shape, value.dtype),
        in_specs=[vmem, pl.BlockSpec(memory_space=pl.ANY)],
        out_specs=vmem,
        compiler_params=pltpu.CompilerParams(vmem_limit_bytes=2**20),
    )(value, after)


def joined_kernel(plane, *refs):
    pieces, told, packed = refs[:-3], refs[-2], refs[-1]
    at = 0
    for piece in pieces:
        told[at : at + piece.shape[0], :] = piece[...]
        at += piece.shape[0]
    rows = packed.shape[1] - 2 * LANES
    facts = (pieces[0].shape[1] - rows) // 2
    packed[...] = jnp.zeros(packed.shape, packed.dtype)
    for part in range(facts // LANES):
        here = slice(part * LANES, (part + 1) * LANES)
        packed[part : part + 1, 0:LANES] = pieces[0][0:1, here]
        packed[part : part + 1, LANES : 2 * LANES] = pieces[0][0:1, facts + part * LANES : facts + (part + 1) * LANES]
    packed[0:plane, 2 * LANES :] = told[0:plane, 2 * facts :]


def joined(pieces, facts, after):
    vmem = pl.BlockSpec(memory_space=pltpu.VMEM)
    length = pieces[0].shape[1]
    plane = sum(p.shape[0] for p in pieces)
    return pl.pallas_call(
        functools.partial(joined_kernel, plane),
        out_shape=[
            jax.ShapeDtypeStruct((plane, length), jnp.float32),
            jax.ShapeDtypeStruct((max(plane, facts // LANES), length - 2 * facts + 2 * LANES), jnp.float32),
        ],
        in_specs=[vmem] * len(pieces) + [pl.BlockSpec(memory_space=pl.ANY)],
        out_specs=[vmem, vmem],
        compiler_params=pltpu.CompilerParams(vmem_limit_bytes=2**20),
    )(*pieces, after)


def device_table(shards, plane, planes, order, place_of, here):
    rel = jnp.arange(shards, dtype=jnp.int32)
    place = jnp.sum(jnp.where(jnp.arange(planes) == here // plane, jnp.asarray(place_of, jnp.int32), 0))
    place = (place - rel // plane) % planes
    z = jnp.sum(jnp.where(place[:, None] == jnp.arange(planes)[None, :], jnp.asarray(order, jnp.int32)[None, :], 0), axis=1)
    return (z * plane + (here % plane ^ rel % plane)).reshape(shards, 1)


def per_device(embeddings, scales, cluster, pair_listed):
    rows, width = embeddings.shape
    shards = lax.axis_size("shard")
    here = lax.axis_index("shard")
    plane = 1
    while plane * plane * 4 <= shards:
        plane *= 2
    planes = shards // plane
    half = planes // 2
    owned, partners = pair_listed.shape

    order = [place // 2 + (place % 2) * half for place in range(planes)]
    place_of = [order.index(z) for z in range(planes)]

    def permuted(value, target):
        return lax.ppermute(value, "shard", [(s, target(s)) for s in range(shards)])

    def across(bit):
        return lambda s: s ^ bit

    def along(distance):
        def target(s):
            z = order[(place_of[s // plane] + distance) % planes]
            return z * plane + s % plane

        return target

    arrived = {}
    for distance in range(1, half + 1):
        arrived[distance] = permuted(embeddings, along(distance))
    parts = 2
    size = rows // parts
    held = {(0, p): embeddings[p * size : (p + 1) * size] for p in range(parts)}
    whole_block = {0: embeddings}
    bit = plane // 2
    while bit:
        for j, p in sorted(held):
            if bit == 1 and j == 0:
                continue
            held[j | bit, p] = permuted(held[j, p], across(bit))
        bit //= 2
    whole_block[1] = permuted(embeddings, across(1))
    blocks = []
    for j in range(plane):
        blocks += [whole_block[j]] if j in whole_block else [held[j, p] for p in range(parts)]

    pairs = jnp.pad(pair_listed.reshape(-1).astype(jnp.float32), (0, -(owned * partners) % LANES))
    told = jnp.concatenate([scales.astype(jnp.float32), cluster[:, 0].astype(jnp.float32), pairs])[None, :]
    told = kept(told, held[plane // 2, 0])
    pieces, bit = [told], 1
    while bit < plane:
        mine = pieces[0] if len(pieces) == 1 else jnp.concatenate(pieces, axis=0)
        pieces.append(permuted(mine, across(bit)))
        bit *= 2
    raw, turned, whole = gathered_plane(blocks)
    told, packed = joined(pieces, rows, raw)
    distant = [permuted(packed, along(t)) for t in range(1, planes)]
    device = device_table(shards, plane, planes, order, place_of, here)
    distances = range(1, half + 1)
    two_sided = [2 * distance != planes for distance in distances]
    own_classes = classes(told, turned, partners)
    given = [raw] + [products(arrived[distance], whole, own_classes) for distance in distances[1:]]
    found = maxima(device, told, own_classes, distant, partners, arrived[1], whole, given, two_sided)
    gathered, columns = found[:plane], list(found[plane:])

    result = gathered[0]
    returned = []
    for distance in distances:
        if two_sided[distance - 1]:
            returned.append(permuted(columns.pop(0), along(-distance)))
    returned += [permuted(gathered[j], across(j)) for j in range(plane - 1, 0, -1)]
    return functools.reduce(jnp.maximum, returned, result).reshape(rows)


def solution(mesh):
    placed = (
        P(("groups", "shard"), None),
        P(("groups", "shard")),
        P(("groups", "shard"), None),
        P(("groups", "shard"), None),
    )
    return jax.shard_map(
        per_device, mesh=mesh, in_specs=placed, out_specs=P(("groups", "shard")), check_vma=False
    )
```
